256 devices in a mesh: station: 64 (over x, z, core), sample: 4 (over y).
Axes of the slice: x: 4, y: 4, z: 8, core: 2. Of those that a mesh axis runs over, the one named last changes fastest.
Arguments:
- flux: bfloat16 [16, 2048, 3584], P('sample', 'station'), may hold values from -6 to 6
- coeff: float32 [2048, 3584], P('station'), may hold values from 0.02 to 0.24
- diff_steps: int32 [16], P('sample'), may hold values from 3 to 6, as said below
- footprint: bfloat16 [1024, 4, 16384], P('station'), may hold values from -0.03125 to 0.03125
- tile_src: int32 [1024, 4, 1], replicated, may hold values from 0 to 63; in each aligned block of 64 rows (0 to 63, 64 to 127, ..., all dimensions but the last counted through in order) at most 2 rows name the same one
- tile_local: int32 [1024, 4], replicated, may hold values from 0 to 6
- tile_count: int32 [1024], P('station'), may hold values from 1 to 4
Outputs:
- observed: float32 [1024, 16], P('station')
The draws below stay inside these ranges and needn't reach their ends.
Inputs may be any that keep to these rules, and one draw needn't show every extreme that they name: `tile_src`: in each aligned block of 64 rows (the slots of one index's stations, stations and slots in order), no band appears more than 2 times, and some band appears exactly 2 times. `diff_steps`: some sample takes 6 steps and another takes 3.
All inputs are finite; a program needn't handle non-finite values.
Results may differ from the reference program's by a relative error of at most 0.0029.
Values may be sent and summed in bfloat16 or wider, within the bound.
No kernel may reach another device: no remote copies, remote signals or barrier semaphores. Data moves between devices by JAX's collectives and lax.ppermute only.
A program may use at most 128 MiB of HBM per device.

```python
import math
import jax
import jax.numpy as jnp
import numpy as np
from jax import lax

STA_DEV = 16
ROWS_DEV = 32
TILE_LON = 512
TILES_DEV = 7
KT = 4
ITERS = 6
TILE = 16384
NLON = 3584
NLAT = 2048
SAMPLES = 16
STATIONS = 1024
CAP = 2
N_STATION = 64


def draw_diff_steps(key, part):
    key_base = jax.random.fold_in(key, 11)
    key_first = jax.random.fold_in(key, 23)
    key_shift = jax.random.fold_in(key, 37)
    steps = jax.random.randint(key_base, (SAMPLES,), 3, ITERS + 1, dtype=jnp.int32)
    first = jax.random.randint(key_first, (), 0, SAMPLES, dtype=jnp.int32)
    shift = jax.random.randint(key_shift, (), 1, SAMPLES, dtype=jnp.int32)
    second = (first + shift) % SAMPLES
    positions = jnp.arange(SAMPLES, dtype=jnp.int32)
    steps = jnp.where(positions == first, ITERS, steps)
    steps = jnp.where(positions == second, 3, steps)
    return steps.astype(jnp.int32)


def with_ends(drawn, own_key, low, largest):
    extent = drawn.shape
    place = [jax.random.randint(jax.random.fold_in(own_key, axis), (), 0, extent[axis]) for axis in range(len(extent))]
    drawn = drawn.at[tuple(place)].set(low)
    longest = extent.index(max(extent))
    place[longest] = (place[longest] + 1) % extent[longest]
    return drawn.at[tuple(place)].set(largest)


def block_scale(key, extent, cuts, smallest, high):
    factor_of, own = 1.0, jax.random.fold_in(key, 6)
    for position, shards_of in cuts:
        steps = jnp.exp(jax.random.uniform(jax.random.fold_in(own, position), (shards_of,), jnp.float32, smallest / len(cuts), high / len(cuts)))
        factor_of = factor_of * jnp.repeat(steps, extent[position] // shards_of).reshape([-1 if axis == position else 1 for axis in range(len(extent))])
    return factor_of


def deal_out(own_key, own, number, rows, count, top, reach, skew):
    order = jax.random.permutation(own_key, count)
    packed, usual = shares(count, rows * top, reach, skew, True), shares(count, rows * top, reach, skew, False)
    places = jnp.arange(count)

    def named(tallies, turn):
        used = int((tallies > 0).sum())
        fixed = max(1, used // 4)
        moved = fixed + (places - fixed + turn * (used - fixed)) % max(1, count - fixed)
        return jnp.zeros((count,), jnp.int32).at[order[jnp.where(places < fixed, places, moved)]].set(jnp.asarray(tallies, jnp.int32))

    tallies = jnp.where(number % 4 == 0, named(packed, number // 4), named(usual, number - number // 4 - 1))
    mixed = jax.random.permutation(jax.random.fold_in(own, 3), count)
    giver, taker = mixed[0:count // 2 * 2:2], mixed[1:count // 2 * 2:2]
    room = jnp.minimum(tallies[giver] - 1, reach - tallies[taker]) // 2
    room = jnp.where((giver == order[0]) | (taker == order[0]) | (tallies[taker] == 0), 0, jnp.maximum(room, 0))
    moved = jax.random.randint(jax.random.fold_in(own, 4), (count // 2,), 0, 1 << 20) % (room + 1)
    tallies = tallies.at[giver].add(-moved).at[taker].add(moved)
    members = jnp.searchsorted(jnp.cumsum(tallies), jnp.arange(rows * top), side="right").astype(jnp.int32)
    grid = members.reshape(top, rows).T
    grid = grid[jax.random.permutation(jax.random.fold_in(own, 1), rows)]
    turn = jax.random.randint(jax.random.fold_in(own, 2), (rows, 1), 0, top)
    return jnp.take_along_axis(grid, (jnp.arange(top)[None, :] + turn) % top, axis=1)


def shares(number_of, total, most, lean, full):
    portions = [(1 << 20) // math.isqrt(rank ** lean) + 1 for rank in range(1, number_of + 1)]
    largest = most if full else min(most, max(-(-total // number_of), total * portions[0] // sum(portions)))
    least = 1 if total - largest >= number_of - 1 else 0
    given, surplus = [largest] + [least] * (number_of - 1), total - largest - least * (number_of - 1)
    while surplus > 0:
        movable = [i for i in range(1, number_of) if given[i] < largest] or [i for i in range(1, number_of) if given[i] < most]
        mass, budget = sum([portions[i] for i in movable]), surplus
        for i in movable:
            more = min(most - given[i], max(1, budget * portions[i] // mass), surplus)
            given[i] = given[i] + more
            surplus = surplus - more
    return np.array(given)


def scatter_about(stream_key, shape, scale, most, cuts=(), kind=jnp.bfloat16):
    result = scale * jax.random.normal(stream_key, shape, jnp.float32)
    if cuts:
        result = result * block_scale(stream_key, shape, cuts, -0.22, 0.18)
    return jnp.clip(result, -most, most).astype(kind)


def setup_inputs(seed: int = 0) -> dict:
    key_list = jax.random.split(jax.random.key(seed), 8)
    flux = scatter_about(key_list[0], (SAMPLES, NLAT, NLON), 1.0, 6.0, ((0, 4), (1, 64)))
    coeff = jnp.clip(jnp.exp(math.log(0.24) - 2.4849066 * jax.random.uniform(key_list[1], (NLAT, NLON), jnp.float32) ** block_scale(key_list[1], (NLAT, NLON), ((0, 64),), -0.2, 0.2)), 0.02, 0.24)
    diff_steps = draw_diff_steps(jax.random.fold_in(key_list[7], 71), 0)
    footprint = scatter_about(key_list[3], (STATIONS, KT, TILE), (TILE * 2) ** -0.5, 0.03125, ((0, 64),))
    tile_src_keys = jax.random.split(jax.random.fold_in(key_list[4], 1), STATIONS * KT // (STA_DEV * KT))
    tile_src_turns = jax.random.permutation(jax.random.fold_in(key_list[4], 3), STATIONS * KT // (STA_DEV * KT))
    tile_src = jax.vmap(lambda own, number: deal_out(jax.random.fold_in(key_list[4], 2), own, number, STA_DEV * KT, N_STATION, 1, CAP, 2))(tile_src_keys, tile_src_turns).reshape((STATIONS, KT, 1))
    tile_local = with_ends(jax.random.randint(key_list[5], (STATIONS, KT), 0, TILES_DEV), jax.random.fold_in(key_list[5], 1), 0, TILES_DEV - 1).astype(jnp.int32)
    tile_count = with_ends(jax.random.randint(key_list[6], (STATIONS,), 1, KT + 1), jax.random.fold_in(key_list[6], 1), 1, KT).astype(jnp.int32)
    return dict(flux=flux, coeff=coeff, diff_steps=diff_steps, footprint=footprint, tile_src=tile_src, tile_local=tile_local, tile_count=tile_count)


def reference(flux, coeff, diff_steps, footprint, tile_src, tile_local, tile_count):
    def diffuse_one(pair):
        sample_field, limit = pair
        field = sample_field.astype(jnp.float32)
        for step_index in range(ITERS):
            gate = (step_index < limit).astype(jnp.float32)
            padded = jnp.pad(field, ((1, 1), (0, 0)))
            lap = padded[:-2] + padded[2:] + jnp.roll(field, 1, 1) + jnp.roll(field, -1, 1) - 4.0 * field
            field = field + gate * coeff * lap
        return field.astype(jnp.bfloat16)

    final = lax.map(diffuse_one, (flux, diff_steps))
    tiles = final.reshape(SAMPLES, N_STATION, ROWS_DEV, TILES_DEV, TILE_LON)
    tiles = tiles.transpose(1, 3, 0, 2, 4).reshape(N_STATION * TILES_DEV, SAMPLES, TILE)

    def station_obs(group):
        prints, sources, locals_, count = group
        ids = (sources[:, 0] * TILES_DEV + locals_).astype(jnp.int32)
        picked = tiles[ids]
        values = jnp.einsum("kst,kt->ks", picked.astype(jnp.float32), prints.astype(jnp.float32))
        live = (jnp.arange(KT, dtype=jnp.int32) < count).astype(jnp.float32)
        return jnp.sum(values * live[:, None], axis=0)

    return lax.map(station_obs, (footprint, tile_src, tile_local, tile_count))
```

```python
import jax
import jax.numpy as jnp
from jax import lax
from jax.experimental import pallas as pl
from jax.experimental.pallas import tpu as pltpu
from jax.sharding import PartitionSpec as P

TILE_LON = 512
TILES_DEV = 7
KT = 4
ITERS = 6
CAP = 2
HALO = 8
PARTS = 4
VMEM = pltpu.VMEM
SMEM = pltpu.SMEM


def spec(space):
    return pl.BlockSpec(memory_space=space)


def pack_kernel(src_ref, prints_ref, sent_ref, place_ref, held_ref, slot_ref):
    slots = prints_ref.shape[0]
    bands = sent_ref.shape[0]

    def clear(i, carry):
        held_ref[i] = 0
        slot_ref[2 * i] = 0
        slot_ref[2 * i + 1] = 0
        return carry

    lax.fori_loop(0, bands, clear, 0)

    def assign(j, carry):
        band = src_ref[j]
        rank = jnp.minimum(held_ref[band], CAP - 1)
        held_ref[band] = rank + 1
        place_ref[j] = CAP * band + rank
        slot_ref[CAP * band + rank] = j
        return carry

    lax.fori_loop(0, slots, assign, 0)

    def fill(i, carry):
        first = prints_ref[slot_ref[2 * i]]
        second = prints_ref[slot_ref[2 * i + 1]]
        sent_ref[i] = jnp.concatenate([first, second], axis=0)
        return carry

    lax.fori_loop(0, bands, fill, 0, unroll=4)


def diffuse_kernel(
    own_ref, steps_ref, flux_ref, above_ref, below_ref, coef_ref, coef_above_ref, coef_below_ref,
    out_ref, field_ref, coefs_ref,
):
    own = own_ref[0]
    samples, rows, lon = flux_ref.shape
    tall = rows + 2 * HALO
    coefs_ref[0:HALO] = coef_above_ref[...]
    coefs_ref[HALO : HALO + rows] = coef_ref[...]
    coefs_ref[HALO + rows :] = coef_below_ref[...]
    edge = jnp.zeros((HALO, lon), jnp.float32)
    for pair in range(samples // 2):
        ends = []
        for side in range(2):
            sample = 2 * pair + side
            for turn in range(2):
                field_ref[side, turn, 0:HALO] = edge
                field_ref[side, turn, HALO + tall :] = edge
            field_ref[side, 0, HALO : 2 * HALO] = above_ref[sample].astype(jnp.float32)
            field_ref[side, 0, 2 * HALO : 2 * HALO + rows] = flux_ref[sample].astype(jnp.float32)
            field_ref[side, 0, 2 * HALO + rows : 3 * HALO + rows] = below_ref[sample].astype(jnp.float32)
            count = jnp.minimum(steps_ref[sample], ITERS)

            def step(k, carry, side=side):
                turn = lax.rem(k, 2)
                for tile in range(tall // 8):
                    at = HALO + 8 * tile
                    center = field_ref[side, turn, at : at + 8]
                    north = field_ref[side, turn, at - 1 : at + 7]
                    south = field_ref[side, turn, at + 1 : at + 9]
                    east = pltpu.roll(center, lon - 1, 1)
                    west = pltpu.roll(center, 1, 1)
                    lap = (north + south + east + west) - 4.0 * center
                    field_ref[side, 1 - turn, at : at + 8] = center + coefs_ref[8 * tile : 8 * tile + 8] * lap
                return carry

            lax.fori_loop(0, count, step, 0)
            ends.append(lax.rem(count, 2))
        for part in range(PARTS):
            at = 2 * HALO + 8 * part
            both = jnp.concatenate([field_ref[side, ends[side], at : at + 8] for side in range(2)], axis=0)
            out_ref[lax.rem(part + PARTS - own, PARTS), 16 * pair : 16 * pair + 16] = both.astype(jnp.bfloat16)


def dots_kernel(own_ref, loc_ref, prints_ref, own_part, part1, part2, part3, out_ref, cells_ref, sums_ref):
    own = own_ref[0]
    bands, _, width = prints_ref.shape
    slots = bands * CAP
    for turn, part in enumerate((own_part, part1, part2, part3)):
        at = pl.multiple_of(lax.rem(own + turn, PARTS) * 32, 32)
        cells_ref[pl.ds(at, 32)] = part[...]
    prints = prints_ref[...].reshape(slots * 8, width)
    for tile in range(TILES_DEV):
        sums = lax.dot_general(
            prints,
            cells_ref[:, tile * width : (tile + 1) * width],
            (((1,), (1,)), ((), ())),
            preferred_element_type=jnp.float32,
        )
        sums_ref[tile] = sums.reshape(slots, 8, 128)
    same = lax.rem(lax.broadcasted_iota(jnp.int32, (8, 128), 1), 8) == lax.broadcasted_iota(jnp.int32, (8, 128), 0)

    def pick(group, carry):
        at = pl.multiple_of(group * 8, 8)
        rows = [
            jnp.sum(jnp.where(same, sums_ref[loc_ref[at + i], at + i], 0.0), axis=0, keepdims=True) for i in range(8)
        ]
        out_ref[pl.ds(at, 8)] = jnp.concatenate(rows, axis=0)
        return carry

    lax.fori_loop(0, slots // 8, pick, 0, unroll=2)


def station_kernel(place_ref, count_ref, back_ref, out_ref, sums_ref):
    stations = sums_ref.shape[0]
    for station in range(stations):
        total = back_ref[pl.ds(place_ref[KT * station], 1)]
        for k in range(1, KT):
            row = back_ref[pl.ds(place_ref[KT * station + k], 1)]
            total = total + jnp.where(k < count_ref[station], row, 0.0)
        sums_ref[station : station + 1] = jnp.where(0 < count_ref[station], total, 0.0)
    lane = lax.broadcasted_iota(jnp.int32, (128, 16), 0)
    sample = lax.broadcasted_iota(jnp.int32, (128, 16), 1)
    fold = (lax.div(lane, 8) == sample).astype(jnp.float32)
    out_ref[...] = jnp.dot(
        sums_ref[...], fold, precision=lax.Precision.HIGHEST, preferred_element_type=jnp.float32
    )


def body(flux, coeff, diff_steps, footprint, tile_src, tile_local, tile_count):
    samples, rows, lon = flux.shape
    stations = footprint.shape[0]
    slots = stations * KT
    bands = lax.axis_size("station")
    band = lax.axis_index("station")
    part = lax.axis_index("sample")
    own = part.astype(jnp.int32).reshape(1)
    cells = rows * TILE_LON // PARTS
    down = [(i, i + 1) for i in range(bands - 1)]
    up = [(i + 1, i) for i in range(bands - 1)]

    above = lax.ppermute(flux[:, rows - HALO :], "station", down)
    below = lax.ppermute(flux[:, :HALO], "station", up)
    coef_above = lax.ppermute(coeff[rows - HALO :], "station", down)
    coef_below = lax.ppermute(coeff[:HALO], "station", up)

    src_all = tile_src.reshape(bands, slots)
    my_src = lax.dynamic_index_in_dim(src_all, band, 0, keepdims=False)
    prints = lax.dynamic_slice_in_dim(footprint, part * cells, cells, axis=2).reshape(slots, 8, TILE_LON)
    sent, place = pl.pallas_call(
        pack_kernel,
        out_shape=(
            jax.ShapeDtypeStruct((bands, 8 * CAP, TILE_LON), jnp.bfloat16),
            jax.ShapeDtypeStruct((slots,), jnp.int32),
        ),
        in_specs=[spec(SMEM), spec(VMEM)],
        out_specs=(spec(VMEM), spec(SMEM)),
        scratch_shapes=[SMEM((bands,), jnp.int32), SMEM((CAP * bands,), jnp.int32)],
        name="pack",
    )(my_src, prints)
    arrived = lax.all_to_all(sent, "station", split_axis=0, concat_axis=0, tiled=True)

    code = jnp.arange(slots, dtype=jnp.int32)[None, :] * 8 + tile_local.reshape(bands, slots)
    mine = src_all == band
    first = jnp.min(jnp.where(mine, code, slots * 8), axis=1)
    last = jnp.max(jnp.where(mine, code, 0), axis=1)
    loc = jnp.stack([first, last], axis=1).reshape(bands * CAP) & 7

    final = pl.pallas_call(
        diffuse_kernel,
        out_shape=jax.ShapeDtypeStruct((PARTS, samples * 8, lon), jnp.bfloat16),
        in_specs=[spec(SMEM), spec(SMEM)] + [spec(VMEM)] * 6,
        out_specs=spec(VMEM),
        scratch_shapes=[
            VMEM((2, 2, rows + 4 * HALO, lon), jnp.float32),
            VMEM((rows + 2 * HALO, lon), jnp.float32),
        ],
        compiler_params=pltpu.CompilerParams(vmem_limit_bytes=24 * 2**20),
        name="diffuse",
    )(own, diff_steps, flux, above, below, coeff, coef_above, coef_below)

    parts = [final[0]] + [
        lax.ppermute(final[turn], "sample", [(i, (i + turn) % PARTS) for i in range(PARTS)]) for turn in (3, 2, 1)
    ]

    values = pl.pallas_call(
        dots_kernel,
        out_shape=jax.ShapeDtypeStruct((bands * CAP, 128), jnp.float32),
        in_specs=[spec(SMEM), spec(SMEM)] + [spec(VMEM)] * 5,
        out_specs=spec(VMEM),
        scratch_shapes=[
            VMEM((samples * 8 * PARTS, lon), jnp.bfloat16),
            VMEM((TILES_DEV, bands * CAP, 8, 128), jnp.float32),
        ],
        compiler_params=pltpu.CompilerParams(vmem_limit_bytes=24 * 2**20),
        name="dots",
    )(own, loc, arrived, *parts)

    back = lax.all_to_all(values.reshape(bands, CAP, 128), "station", split_axis=0, concat_axis=0, tiled=True)
    share = pl.pallas_call(
        station_kernel,
        out_shape=jax.ShapeDtypeStruct((stations, 16), jnp.float32),
        in_specs=[spec(SMEM), spec(SMEM), spec(VMEM)],
        out_specs=spec(VMEM),
        scratch_shapes=[VMEM((stations, 128), jnp.float32)],
        name="stations",
    )(place, tile_count, back.reshape(bands * CAP, 128))
    others = [lax.ppermute(share, "sample", [(i, i ^ flip) for i in range(PARTS)]) for flip in (1, 2, 3)]
    return (share + others[0]) + (others[1] + others[2])


def solution(mesh):
    in_specs = (
        P("sample", "station", None),
        P("station", None),
        P("sample"),
        P("station", None, None),
        P(),
        P(),
        P("station"),
    )
    return jax.shard_map(body, mesh=mesh, in_specs=in_specs, out_specs=P("station", None), check_vma=False)
```

```python
import jax
import jax.numpy as jnp
from jax import lax
from jax.experimental import pallas as pl
from jax.experimental.pallas import tpu as pltpu
from jax.sharding import PartitionSpec as P

TILE_LON = 512
TILES_DEV = 7
KT = 4
ITERS = 6
CAP = 2
HALO = 8
PARTS = 4
CORES = 2
LANES = 128
VMEM = pltpu.VMEM
SMEM = pltpu.SMEM


def spec(space):
    return pl.BlockSpec(memory_space=space)


def pack_kernel(src_ref, prints_ref, sent_ref, place_ref, held_ref, slot_ref):
    slots = prints_ref.shape[0]
    bands = sent_ref.shape[0]

    def clear(i, carry):
        held_ref[i] = 0
        slot_ref[2 * i] = 0
        slot_ref[2 * i + 1] = 0
        return carry

    lax.fori_loop(0, bands, clear, 0, unroll=8)

    def assign(station, carry):
        for k in range(KT):
            band = src_ref[k, station]
            rank = jnp.minimum(held_ref[band], CAP - 1)
            held_ref[band] = rank + 1
            place_ref[KT * station + k] = CAP * band + rank
            slot_ref[CAP * band + rank] = KT * station + k
        return carry

    lax.fori_loop(0, slots // KT, assign, 0)

    def fill(i, carry):
        first = prints_ref[slot_ref[2 * i]]
        second = prints_ref[slot_ref[2 * i + 1]]
        sent_ref[i] = jnp.concatenate([first, second], axis=0)
        return carry

    lax.fori_loop(0, bands, fill, 0, unroll=8)


def diffuse_kernel(
    own_ref, steps_ref, flux_ref, above_ref, below_ref, coef_ref,
    out0_ref, out1_ref, out2_ref, out3_ref, field_ref, coefs_ref,
):
    own = own_ref[0]
    samples, rows, lon = flux_ref.shape
    strips = lon // LANES
    tall = rows + 2 * HALO
    edge = jnp.zeros((HALO, LANES), jnp.float32)
    lane = lax.broadcasted_iota(jnp.int32, (8, LANES), 1)
    first_lane = lane == 0
    last_lane = lane == LANES - 1

    for strip in range(strips):
        at = slice(strip * LANES, (strip + 1) * LANES)
        for ref, low in ((above_ref, 0), (below_ref, HALO + rows)):
            coefs_ref[strip, low : low + HALO] = ref[samples, :, at].astype(jnp.float32) + ref[
                samples + 1, :, at
            ].astype(jnp.float32)
        coefs_ref[strip, HALO : HALO + rows] = coef_ref[:, at]

    def evolve(sample, carry):
        for strip in range(strips):
            at = slice(strip * LANES, (strip + 1) * LANES)
            for turn in range(2):
                field_ref[sample, turn, strip, 0:HALO] = edge
                field_ref[sample, turn, strip, HALO + tall :] = edge
            field_ref[sample, 0, strip, HALO : 2 * HALO] = above_ref[sample, :, at].astype(jnp.float32)
            field_ref[sample, 0, strip, 2 * HALO : 2 * HALO + rows] = flux_ref[sample, :, at].astype(jnp.float32)
            field_ref[sample, 0, strip, 2 * HALO + rows : HALO + tall] = below_ref[sample, :, at].astype(jnp.float32)
        count = jnp.minimum(steps_ref[sample], ITERS)

        def step(k, carry):
            turn = lax.rem(k, 2)

            def update(tile):
                at = HALO + 8 * tile

                def load(strip):
                    return field_ref[sample, turn, strip % strips, at : at + 8]

                before = pltpu.roll(load(strips - 1), 1, 1)
                center = load(0)
                ahead = pltpu.roll(center, LANES - 1, 1)
                for strip in range(strips):
                    behind = pltpu.roll(center, 1, 1)
                    following = load(strip + 1)
                    after = pltpu.roll(following, LANES - 1, 1)
                    west = jnp.where(first_lane, before, behind)
                    east = jnp.where(last_lane, after, ahead)
                    north = field_ref[sample, turn, strip, at - 1 : at + 7]
                    south = field_ref[sample, turn, strip, at + 1 : at + 9]
                    lap = (north + south + east + west) - 4.0 * center
                    coefs = coefs_ref[strip, 8 * tile : 8 * tile + 8]
                    field_ref[sample, 1 - turn, strip, at : at + 8] = center + coefs * lap
                    before, center, ahead = behind, following, after

            @pl.when(k < count - 1)
            def _():
                update(0)
                update(tall // 8 - 1)

            for tile in range(1, tall // 8 - 1):
                update(tile)
            return carry

        lax.fori_loop(0, count, step, 0)
        return carry

    lax.fori_loop(0, samples, evolve, 0)

    for turn, out_ref in enumerate((out0_ref, out1_ref, out2_ref, out3_ref)):
        part = lax.rem(own + turn, PARTS)
        low = pl.multiple_of(2 * HALO + 8 * part, 8)
        for pair in range(samples // 2):
            ends = [lax.rem(jnp.minimum(steps_ref[2 * pair + side], ITERS), 2) for side in range(2)]
            for strip in range(strips):
                both = [field_ref[2 * pair + side, ends[side], strip, pl.ds(low, 8)] for side in range(2)]
                out_ref[16 * pair : 16 * pair + 16, strip * LANES : (strip + 1) * LANES] = jnp.concatenate(
                    both, axis=0
                ).astype(jnp.bfloat16)


def gather_kernel(own_ref, *refs):
    own = own_ref[0]
    cells_ref = refs[-1]
    for core in range(CORES):
        for turn in range(PARTS):
            low = pl.multiple_of(lax.rem(own + turn, PARTS) * 32, 32)
            for tile in range(TILES_DEV):
                part = refs[core * PARTS + turn][:, tile * TILE_LON : (tile + 1) * TILE_LON]
                cells_ref[core, tile, pl.ds(low, 32)] = part
        cells_ref[core, TILES_DEV] = jnp.zeros(cells_ref.shape[2:], jnp.bfloat16)


def dots_kernel(loc_ref, prints_ref, cells_ref, out_ref, sums_ref):
    peers, _, width = prints_ref.shape
    for core in range(CORES):
        prints = prints_ref[:, 16 * core : 16 * core + 16].reshape(peers * 16, width)
        for two in range((TILES_DEV + 1) // 2):
            sums = lax.dot_general(
                prints,
                cells_ref[core, 2 * two : 2 * two + 2].reshape(2 * LANES, width),
                (((1,), (1,)), ((), ())),
                preferred_element_type=jnp.float32,
            )
            for side in range(2):
                if 2 * two + side < TILES_DEV:
                    sums_ref[core, 2 * two + side] = sums[:, side * LANES : (side + 1) * LANES].reshape(
                        peers, CAP, 8, LANES
                    )
    same = lax.rem(lax.broadcasted_iota(jnp.int32, (8, LANES), 1), 8) == lax.broadcasted_iota(
        jnp.int32, (8, LANES), 0
    )

    def pick(two, carry):
        rows = []
        for i in range(2):
            peer = 2 * two + i
            for core in range(CORES):
                for slot in range(CAP):
                    loc = loc_ref[(peer * CORES + core) * CAP + slot]
                    rows.append(
                        jnp.sum(jnp.where(same, sums_ref[core, loc, peer, slot], 0.0), axis=0, keepdims=True)
                    )
        out_ref[pl.ds(pl.multiple_of(two * 8, 8), 8)] = jnp.concatenate(rows, axis=0)
        return carry

    lax.fori_loop(0, peers // 2, pick, 0, unroll=2)


def station_kernel(place_ref, count_ref, back_ref, out_ref, sums_ref):
    stations = sums_ref.shape[0]
    for station in range(stations):
        total = back_ref[pl.ds(place_ref[KT * station], 1)]
        for k in range(1, KT):
            row = back_ref[pl.ds(place_ref[KT * station + k], 1)]
            total = total + jnp.where(k < count_ref[station], row, 0.0)
        sums_ref[station : station + 1] = jnp.where(0 < count_ref[station], total, 0.0)
    lane = lax.broadcasted_iota(jnp.int32, (LANES, 16), 0)
    sample = lax.broadcasted_iota(jnp.int32, (LANES, 16), 1)
    fold = (lax.div(lane, 8) == sample).astype(jnp.float32)
    out_ref[...] = jnp.dot(
        sums_ref[...], fold, precision=lax.Precision.HIGHEST, preferred_element_type=jnp.float32
    )


def edge_rows(flux, coeff, low):
    coef = coeff[low : low + HALO]
    head = lax.reduce_precision(coef, 8, 7)
    parts = jnp.stack([head, coef - head]).astype(jnp.bfloat16)
    return jnp.concatenate([flux[:, low : low + HALO], parts], axis=0)


def body(flux, coeff, diff_steps, footprint, tile_src, tile_local, tile_count):
    samples, rows, lon = flux.shape
    stations = footprint.shape[0]
    slots = stations * KT
    bands = lax.axis_size("station")
    peers = bands // CORES
    band = lax.axis_index("station")
    part = lax.axis_index("sample")
    own = part.astype(jnp.int32).reshape(1)
    cells = rows * TILE_LON // PARTS
    down = [(i, i + 1) for i in range(bands - 1)]
    up = [(i + 1, i) for i in range(bands - 1)]
    beside = [(i, i ^ 1) for i in range(bands)]
    same_core = [[CORES * i + core for i in range(peers)] for core in range(CORES)]

    above = lax.ppermute(edge_rows(flux, coeff, rows - HALO), "station", down)
    below = lax.ppermute(edge_rows(flux, coeff, 0), "station", up)

    src_all = tile_src[:, :, 0].T
    my_src = lax.dynamic_slice_in_dim(src_all, band * stations, stations, axis=1)
    prints = lax.dynamic_slice_in_dim(footprint, part * cells, cells, axis=2).reshape(slots, 8, TILE_LON)
    sent, place = pl.pallas_call(
        pack_kernel,
        out_shape=(
            jax.ShapeDtypeStruct((bands, 8 * CAP, TILE_LON), jnp.bfloat16),
            jax.ShapeDtypeStruct((slots,), jnp.int32),
        ),
        in_specs=[spec(SMEM), spec(VMEM)],
        out_specs=(spec(VMEM), spec(SMEM)),
        scratch_shapes=[SMEM((bands,), jnp.int32), SMEM((CAP * bands,), jnp.int32)],
        name="pack",
    )(my_src, prints)
    arrived = lax.all_to_all(
        sent.reshape(peers, CORES * CAP * 8, TILE_LON),
        "station", split_axis=0, concat_axis=0, axis_index_groups=same_core, tiled=True,
    )

    finals = pl.pallas_call(
        diffuse_kernel,
        out_shape=[jax.ShapeDtypeStruct((samples * 8, lon), jnp.bfloat16)] * PARTS,
        in_specs=[spec(SMEM), spec(SMEM)] + [spec(VMEM)] * 4,
        out_specs=[spec(VMEM)] * PARTS,
        scratch_shapes=[
            VMEM((samples, 2, lon // LANES, rows + 4 * HALO, LANES), jnp.float32),
            VMEM((lon // LANES, rows + 2 * HALO, LANES), jnp.float32),
        ],
        compiler_params=pltpu.CompilerParams(vmem_limit_bytes=28 * 2**20),
        name="diffuse",
    )(own, diff_steps, flux, above, below, coeff)
    parts = [finals[0]] + [
        lax.ppermute(finals[turn], "sample", [(i, (i + turn) % PARTS) for i in range(PARTS)]) for turn in (3, 2, 1)
    ]
    theirs = [lax.ppermute(each, "station", beside) for each in parts]
    core = lax.rem(band, CORES)
    lower = [jnp.where(core == 0, a, b) for a, b in zip(parts, theirs)]
    upper = [jnp.where(core == 0, b, a) for a, b in zip(parts, theirs)]
    tiles = pl.pallas_call(
        gather_kernel,
        out_shape=jax.ShapeDtypeStruct((CORES, TILES_DEV + 1, LANES, TILE_LON), jnp.bfloat16),
        in_specs=[spec(SMEM)] + [spec(VMEM)] * (CORES * PARTS),
        out_specs=spec(VMEM),
        compiler_params=pltpu.CompilerParams(vmem_limit_bytes=24 * 2**20),
        name="tiles",
    )(own, *lower, *upper)

    order = jnp.arange(stations * bands, dtype=jnp.int32) % stations
    code = (order[None, :] * KT + jnp.arange(KT, dtype=jnp.int32)[:, None]) * 8 + tile_local.T
    picks = []
    for side in range(CORES):
        mine = src_all == (band - core + side)
        first = jnp.min(jnp.min(jnp.where(mine, code, slots * 8), axis=0).reshape(bands, stations), axis=1)
        last = jnp.max(jnp.max(jnp.where(mine, code, 0), axis=0).reshape(bands, stations), axis=1)
        picks += [first & 7, last & 7]
    loc = lax.dynamic_index_in_dim(jnp.stack(picks, axis=1).reshape(peers, CORES, CORES * CAP), core, 1, keepdims=False)

    values = pl.pallas_call(
        dots_kernel,
        out_shape=jax.ShapeDtypeStruct((bands * CAP, LANES), jnp.float32),
        in_specs=[spec(SMEM), spec(VMEM), spec(VMEM)],
        out_specs=spec(VMEM),
        scratch_shapes=[VMEM((CORES, TILES_DEV, peers, CAP, 8, LANES), jnp.float32)],
        compiler_params=pltpu.CompilerParams(vmem_limit_bytes=24 * 2**20),
        name="dots",
    )(loc.reshape(-1), arrived, tiles)

    back = lax.all_to_all(
        values.reshape(peers, CORES * CAP, LANES),
        "station", split_axis=0, concat_axis=0, axis_index_groups=same_core, tiled=True,
    )
    share = pl.pallas_call(
        station_kernel,
        out_shape=jax.ShapeDtypeStruct((stations, 16), jnp.float32),
        in_specs=[spec(SMEM), spec(SMEM), spec(VMEM)],
        out_specs=spec(VMEM),
        scratch_shapes=[VMEM((stations, LANES), jnp.float32)],
        name="stations",
    )(place, tile_count, back.reshape(bands * CAP, LANES))
    others = [lax.ppermute(share, "sample", [(i, i ^ flip) for i in range(PARTS)]) for flip in (1, 2, 3)]
    return (share + others[0]) + (others[1] + others[2])


def solution(mesh):
    in_specs = (
        P("sample", "station", None),
        P("station", None),
        P("sample"),
        P("station", None, None),
        P(),
        P(),
        P("station"),
    )
    return jax.shard_map(body, mesh=mesh, in_specs=in_specs, out_specs=P("station", None), check_vma=False)
```

```python
import functools

import jax
import jax.numpy as jnp
from jax import lax
from jax.experimental import pallas as pl
from jax.experimental.pallas import tpu as pltpu
from jax.sharding import PartitionSpec as P

TILE_LON = 512
TILES_DEV = 7
KT = 4
ITERS = 6
CAP = 2
HALO = 8
PARTS = 4
CORES = 2
LANES = 128
VMEM = pltpu.VMEM
SMEM = pltpu.SMEM


def spec(space):
    return pl.BlockSpec(memory_space=space)


def pack_kernel(src_ref, prints_ref, sent_ref, place_ref, held_ref, slot_ref):
    slots = prints_ref.shape[0]
    bands = sent_ref.shape[0]

    def clear(i, carry):
        held_ref[i] = 0
        slot_ref[2 * i] = 0
        slot_ref[2 * i + 1] = 0
        return carry

    lax.fori_loop(0, bands, clear, 0, unroll=8)

    def assign(station, carry):
        for k in range(KT):
            band = src_ref[k, station]
            rank = jnp.minimum(held_ref[band], CAP - 1)
            held_ref[band] = rank + 1
            place_ref[KT * station + k] = CAP * band + rank
            slot_ref[CAP * band + rank] = KT * station + k
        return carry

    lax.fori_loop(0, slots // KT, assign, 0)

    def fill(i, carry):
        first = prints_ref[slot_ref[2 * i]]
        second = prints_ref[slot_ref[2 * i + 1]]
        sent_ref[i] = jnp.concatenate([first, second], axis=0)
        return carry

    lax.fori_loop(0, bands, fill, 0, unroll=8)


def edge_kernel(flux_ref, coef_ref, last_ref, first_ref):
    samples, rows, _ = flux_ref.shape
    for ref, low in ((last_ref, rows - HALO), (first_ref, 0)):
        ref[0:samples] = flux_ref[:, low : low + HALO]
        coef = coef_ref[low : low + HALO]
        head = coef.astype(jnp.bfloat16)
        ref[samples] = head
        ref[samples + 1] = (coef - head.astype(jnp.float32)).astype(jnp.bfloat16)


def diffuse_kernel(
    pair, own_ref, steps_ref, flux_ref, above_ref, below_ref, coef_ref,
    out0_ref, out1_ref, out2_ref, out3_ref, even_ref, odd_ref, coefs_ref,
):
    own = own_ref[0]
    samples, rows, lon = flux_ref.shape
    strips = lon // LANES
    tall = rows + 2 * HALO
    edge = jnp.zeros((HALO, LANES), jnp.float32)
    lane = lax.broadcasted_iota(jnp.int32, (8, LANES), 1)
    first_lane = lane == 0
    last_lane = lane == LANES - 1

    for strip in range(strips):
        at = slice(strip * LANES, (strip + 1) * LANES)
        for ref, low in ((above_ref, 0), (below_ref, HALO + rows)):
            coefs_ref[strip, low : low + HALO] = ref[samples, :, at].astype(jnp.float32) + ref[
                samples + 1, :, at
            ].astype(jnp.float32)
        coefs_ref[strip, HALO : HALO + rows] = coef_ref[:, at]
        for low in (0, HALO + tall):
            odd_ref[strip, low : low + HALO] = edge
            for side in range(2):
                even_ref[side, strip, low : low + HALO] = edge

    def update(old_ref, new_ref, tile):
        at = HALO + 8 * tile

        def load(strip):
            return old_ref[strip % strips, at : at + 8]

        before = pltpu.roll(load(strips - 1), 1, 1)
        center = load(0)
        ahead = pltpu.roll(center, LANES - 1, 1)
        for strip in range(strips):
            behind = pltpu.roll(center, 1, 1)
            following = load(strip + 1)
            after = pltpu.roll(following, LANES - 1, 1)
            west = jnp.where(first_lane, before, behind)
            east = jnp.where(last_lane, after, ahead)
            north = old_ref[strip, at - 1 : at + 7]
            south = old_ref[strip, at + 1 : at + 9]
            lap = (north + south + east + west) - 4.0 * center
            new_ref[strip, at : at + 8] = center + coefs_ref[strip, 8 * tile : 8 * tile + 8] * lap
            before, center, ahead = behind, following, after

    def step(old_ref, new_ref, last):
        @pl.when(jnp.logical_not(last))
        def _():
            update(old_ref, new_ref, 0)
            update(old_ref, new_ref, tall // 8 - 1)

        for tile in range(1, tall // 8 - 1):
            update(old_ref, new_ref, tile)

    def begin(sample, ref):
        for strip in range(strips):
            at = slice(strip * LANES, (strip + 1) * LANES)
            ref[strip, HALO : 2 * HALO] = above_ref[sample, :, at].astype(jnp.float32)
            ref[strip, 2 * HALO : 2 * HALO + rows] = flux_ref[sample, :, at].astype(jnp.float32)
            ref[strip, 2 * HALO + rows : HALO + tall] = below_ref[sample, :, at].astype(jnp.float32)

    def evolve(side, carry):
        sample = 2 * pair + side
        even = even_ref.at[side]
        count = jnp.minimum(steps_ref[sample], ITERS)
        half = lax.div(count, 2)

        @pl.when(lax.rem(count, 2) == 1)
        def _():
            begin(sample, odd_ref)
            step(odd_ref, even, half == 0)

        @pl.when(lax.rem(count, 2) == 0)
        def _():
            begin(sample, even)

        def two(k, carry):
            step(even, odd_ref, False)
            step(odd_ref, even, k == half - 1)
            return carry

        lax.fori_loop(0, half, two, 0)
        return carry

    lax.fori_loop(0, 2, evolve, 0)

    for turn, out_ref in enumerate((out0_ref, out1_ref, out2_ref, out3_ref)):
        low = pl.multiple_of(2 * HALO + 8 * lax.rem(own + turn, PARTS), 8)
        for strip in range(strips):
            both = [even_ref[side, strip, pl.ds(low, 8)] for side in range(2)]
            out_ref[:, strip * LANES : (strip + 1) * LANES] = jnp.concatenate(both, axis=0).astype(jnp.bfloat16)


def dots_kernel(own_ref, core_ref, loc_ref, prints_ref, *refs):
    parts = refs[: CORES * PARTS * 2]
    out_ref, sums_ref = refs[CORES * PARTS * 2 :]
    peers, _, width = prints_ref.shape
    core = core_ref[0]
    each = PARTS * 2
    for group in range(CORES):
        side = core if group == 0 else 1 - core
        prints = prints_ref[:, pl.ds(pl.multiple_of(16 * side, 16), 16)].reshape(peers * 16, width)
        for low in range(0, TILES_DEV, 2):
            tiles = range(low, min(low + 2, TILES_DEV))
            cells = jnp.concatenate(
                [
                    part[:, tile * width : (tile + 1) * width]
                    for tile in tiles
                    for part in parts[group * each : (group + 1) * each]
                ],
                axis=0,
            )
            sums = lax.dot_general(prints, cells, (((1,), (1,)), ((), ())), preferred_element_type=jnp.float32)
            for i, tile in enumerate(tiles):
                sums_ref[group, tile] = sums[:, i * LANES : (i + 1) * LANES].reshape(peers, CAP, 8, LANES)
    same = lax.rem(lax.broadcasted_iota(jnp.int32, (8, LANES), 1), 8) == lax.broadcasted_iota(
        jnp.int32, (8, LANES), 0
    )
    shift = 32 * own_ref[0]

    def pick(two, carry):
        rows = []
        for i in range(2):
            peer = 2 * two + i
            for side in range(CORES):
                group = jnp.where(core == side, 0, 1)
                for slot in range(CAP):
                    loc = loc_ref[(peer * CORES + side) * CAP + slot]
                    rows.append(
                        jnp.sum(jnp.where(same, sums_ref[group, loc, peer, slot], 0.0), axis=0, keepdims=True)
                    )
        out_ref[pl.ds(pl.multiple_of(two * 8, 8), 8)] = pltpu.roll(jnp.concatenate(rows, axis=0), shift, 1)
        return carry

    lax.fori_loop(0, peers // 2, pick, 0, unroll=2)


def station_kernel(place_ref, count_ref, back_ref, out_ref, sums_ref):
    stations = sums_ref.shape[0]
    for station in range(stations):
        total = back_ref[pl.ds(place_ref[KT * station], 1)]
        for k in range(1, KT):
            row = back_ref[pl.ds(place_ref[KT * station + k], 1)]
            total = total + jnp.where(k < count_ref[station], row, 0.0)
        sums_ref[station : station + 1] = jnp.where(0 < count_ref[station], total, 0.0)
    lane = lax.broadcasted_iota(jnp.int32, (LANES, 16), 0)
    sample = lax.broadcasted_iota(jnp.int32, (LANES, 16), 1)
    fold = (lax.div(lane, 8) == sample).astype(jnp.float32)
    out_ref[...] = jnp.dot(
        sums_ref[...], fold, precision=lax.Precision.HIGHEST, preferred_element_type=jnp.float32
    )


def body(flux, coeff, diff_steps, footprint, tile_src, tile_local, tile_count):
    samples, rows, lon = flux.shape
    stations = footprint.shape[0]
    slots = stations * KT
    bands = lax.axis_size("station")
    peers = bands // CORES
    band = lax.axis_index("station")
    part = lax.axis_index("sample")
    own = part.astype(jnp.int32).reshape(1)
    cells = rows * TILE_LON // PARTS
    down = [(i, i + 1) for i in range(bands - 1)]
    up = [(i + 1, i) for i in range(bands - 1)]
    beside = [(i, i ^ 1) for i in range(bands)]
    same_core = [[CORES * i + core for i in range(peers)] for core in range(CORES)]

    last, first = pl.pallas_call(
        edge_kernel,
        out_shape=[jax.ShapeDtypeStruct((samples + 2, HALO, lon), jnp.bfloat16)] * 2,
        in_specs=[spec(VMEM)] * 2,
        out_specs=[spec(VMEM)] * 2,
        name="edges",
    )(flux, coeff)
    above = lax.ppermute(last, "station", down)
    below = lax.ppermute(first, "station", up)

    src_all = tile_src[:, :, 0].T
    my_src = lax.dynamic_slice_in_dim(src_all, band * stations, stations, axis=1)
    prints = lax.dynamic_slice_in_dim(footprint, part * cells, cells, axis=2).reshape(slots, 8, TILE_LON)
    sent, place = pl.pallas_call(
        pack_kernel,
        out_shape=(
            jax.ShapeDtypeStruct((bands, 8 * CAP, TILE_LON), jnp.bfloat16),
            jax.ShapeDtypeStruct((slots,), jnp.int32),
        ),
        in_specs=[spec(SMEM), spec(VMEM)],
        out_specs=(spec(VMEM), spec(SMEM)),
        scratch_shapes=[SMEM((bands,), jnp.int32), SMEM((CAP * bands,), jnp.int32)],
        name="pack",
    )(my_src, prints)
    sent, _, _ = lax.optimization_barrier((sent, above, below))
    arrived = lax.all_to_all(
        sent.reshape(peers, CORES * CAP * 8, TILE_LON),
        "station", split_axis=0, concat_axis=0, axis_index_groups=same_core, tiled=True,
    )

    core = lax.rem(band, CORES).astype(jnp.int32)
    mine, theirs = [None] * (2 * PARTS), [None] * (2 * PARTS)
    for pair in range(samples // 2):
        finals = pl.pallas_call(
            functools.partial(diffuse_kernel, pair),
            out_shape=[jax.ShapeDtypeStruct((16, lon), jnp.bfloat16)] * PARTS,
            in_specs=[spec(SMEM), spec(SMEM)] + [spec(VMEM)] * 4,
            out_specs=[spec(VMEM)] * PARTS,
            scratch_shapes=[
                VMEM((2, lon // LANES, rows + 4 * HALO, LANES), jnp.float32),
                VMEM((lon // LANES, rows + 4 * HALO, LANES), jnp.float32),
                VMEM((lon // LANES, rows + 2 * HALO, LANES), jnp.float32),
            ],
            compiler_params=pltpu.CompilerParams(vmem_limit_bytes=24 * 2**20),
            name="diffuse",
        )(own, diff_steps, flux, above, below, coeff)
        for j in range(PARTS):
            turn = (PARTS - j) % PARTS
            part_j = finals[0]
            if turn:
                part_j = lax.ppermute(finals[turn], "sample", [(i, (i + turn) % PARTS) for i in range(PARTS)])
            mine[2 * j + pair] = part_j
            theirs[2 * j + pair] = lax.ppermute(part_j, "station", beside)

    order = jnp.arange(stations * bands, dtype=jnp.int32) % stations
    code = (order[None, :] * KT + jnp.arange(KT, dtype=jnp.int32)[:, None]) * 8 + tile_local.T
    picks = []
    for side in range(CORES):
        named = src_all == (band - core + side)
        first = jnp.min(jnp.min(jnp.where(named, code, slots * 8), axis=0).reshape(bands, stations), axis=1)
        last = jnp.max(jnp.max(jnp.where(named, code, 0), axis=0).reshape(bands, stations), axis=1)
        picks += [first & 7, last & 7]
    loc = lax.dynamic_index_in_dim(jnp.stack(picks, axis=1).reshape(peers, CORES, CORES * CAP), core, 1, keepdims=False)

    values = pl.pallas_call(
        dots_kernel,
        out_shape=jax.ShapeDtypeStruct((bands * CAP, LANES), jnp.float32),
        in_specs=[spec(SMEM)] * 3 + [spec(VMEM)] * (1 + 2 * CORES * PARTS),
        out_specs=spec(VMEM),
        scratch_shapes=[VMEM((CORES, TILES_DEV, peers, CAP, 8, LANES), jnp.float32)],
        compiler_params=pltpu.CompilerParams(vmem_limit_bytes=24 * 2**20),
        name="dots",
    )(own, core.reshape(1), loc.reshape(-1), arrived, *mine, *theirs)

    back = lax.all_to_all(
        values.reshape(peers, CORES * CAP, LANES),
        "station", split_axis=0, concat_axis=0, axis_index_groups=same_core, tiled=True,
    )
    share = pl.pallas_call(
        station_kernel,
        out_shape=jax.ShapeDtypeStruct((stations, 16), jnp.float32),
        in_specs=[spec(SMEM), spec(SMEM), spec(VMEM)],
        out_specs=spec(VMEM),
        scratch_shapes=[VMEM((stations, LANES), jnp.float32)],
        name="stations",
    )(place, tile_count, back.reshape(bands * CAP, LANES))
    others = [lax.ppermute(share, "sample", [(i, i ^ flip) for i in range(PARTS)]) for flip in (1, 2, 3)]
    return (share + others[0]) + (others[1] + others[2])


def solution(mesh):
    in_specs = (
        P("sample", "station", None),
        P("station", None),
        P("sample"),
        P("station", None, None),
        P(),
        P(),
        P("station"),
    )
    return jax.shard_map(body, mesh=mesh, in_specs=in_specs, out_specs=P("station", None), check_vma=False)
```

```python
import functools

import jax
import jax.numpy as jnp
from jax import lax
from jax.experimental import pallas as pl
from jax.experimental.pallas import tpu as pltpu
from jax.sharding import PartitionSpec as P

TILE_LON = 512
TILES_DEV = 7
KT = 4
ITERS = 6
CAP = 2
HALO = 8
PARTS = 4
LANES = 128
VMEM = pltpu.VMEM
SMEM = pltpu.SMEM


def spec(space):
    return pl.BlockSpec(memory_space=space)


def pack_kernel(part_ref, src_ref, prints_ref, sent_ref, place_ref, held_ref, slot_ref, hot_ref):
    bands, _, width = sent_ref.shape
    stations = prints_ref.shape[0]
    slots = stations * KT

    def clear(i, carry):
        held_ref[i] = 0
        for rank in range(CAP):
            slot_ref[CAP * i + rank] = -(1 << 20)
        return carry

    lax.fori_loop(0, bands, clear, 0, unroll=8)

    def assign(station, carry):
        for k in range(KT):
            band = src_ref[k, station]
            rank = jnp.minimum(held_ref[band], CAP - 1)
            held_ref[band] = rank + 1
            place_ref[KT * station + k] = CAP * band + rank
            slot_ref[CAP * band + rank] = KT * station + k
        return carry

    lax.fori_loop(0, stations, assign, 0)

    row = lax.broadcasted_iota(jnp.int32, (8, width), 0)
    offset = lax.broadcasted_iota(jnp.int32, (8, width), 1) - slots * row

    def heat(i, carry):
        rows = [jnp.where(offset == slot_ref[CAP * i + rank], 1.0, 0.0) for rank in range(CAP)]
        hot_ref[i] = jnp.concatenate(rows, axis=0).astype(jnp.bfloat16)
        return carry

    lax.fori_loop(0, bands, heat, 0, unroll=8)

    flat = prints_ref[...].reshape(slots, 8 * width)
    cells = jnp.concatenate([flat[:, r * width : (r + 1) * width] for r in range(8)], axis=0)
    some = bands // 4
    for low in range(0, bands, some):
        hot = hot_ref[low : low + some].reshape(some * 16, slots * 8)
        moved = jnp.dot(hot, cells, preferred_element_type=jnp.float32).astype(jnp.bfloat16)
        sent_ref[low : low + some] = moved.reshape(some, 16, width)


def edge_kernel(flux_ref, coef_ref, last_ref, first_ref):
    samples, rows, _ = flux_ref.shape
    for ref, low in ((last_ref, rows - HALO), (first_ref, 0)):
        ref[0:samples] = flux_ref[:, low : low + HALO]
        coef = coef_ref[low : low + HALO]
        head = coef.astype(jnp.bfloat16)
        ref[samples] = head
        ref[samples + 1] = (coef - head.astype(jnp.float32)).astype(jnp.bfloat16)


def diffuse_kernel(
    pair, own_ref, steps_ref, flux_ref, above_ref, below_ref, coef_ref,
    out0_ref, out1_ref, out2_ref, out3_ref, even_ref, odd_ref, coefs_ref,
):
    own = own_ref[0]
    samples, rows, lon = flux_ref.shape
    strips = lon // LANES
    tall = rows + 2 * HALO
    edge = jnp.zeros((HALO, LANES), jnp.float32)
    lane = lax.broadcasted_iota(jnp.int32, (8, LANES), 1)
    first_lane = lane == 0
    last_lane = lane == LANES - 1

    for strip in range(strips):
        at = slice(strip * LANES, (strip + 1) * LANES)
        for ref, low in ((above_ref, 0), (below_ref, HALO + rows)):
            coefs_ref[strip, low : low + HALO] = ref[samples, :, at].astype(jnp.float32) + ref[
                samples + 1, :, at
            ].astype(jnp.float32)
        coefs_ref[strip, HALO : HALO + rows] = coef_ref[:, at]
        for low in (0, HALO + tall):
            odd_ref[strip, low : low + HALO] = edge
            for side in range(2):
                even_ref[side, strip, low : low + HALO] = edge

    def update(old_ref, new_ref, tile):
        at = HALO + 8 * tile

        def load(strip):
            return old_ref[strip % strips, at : at + 8]

        before = pltpu.roll(load(strips - 1), 1, 1)
        center = load(0)
        ahead = pltpu.roll(center, LANES - 1, 1)
        for strip in range(strips):
            behind = pltpu.roll(center, 1, 1)
            following = load(strip + 1)
            after = pltpu.roll(following, LANES - 1, 1)
            west = jnp.where(first_lane, before, behind)
            east = jnp.where(last_lane, after, ahead)
            north = old_ref[strip, at - 1 : at + 7]
            south = old_ref[strip, at + 1 : at + 9]
            lap = (north + south + east + west) - 4.0 * center
            new_ref[strip, at : at + 8] = center + coefs_ref[strip, 8 * tile : 8 * tile + 8] * lap
            before, center, ahead = behind, following, after

    def step(old_ref, new_ref, last):
        @pl.when(jnp.logical_not(last))
        def _():
            update(old_ref, new_ref, 0)
            update(old_ref, new_ref, tall // 8 - 1)

        for tile in range(1, tall // 8 - 1):
            update(old_ref, new_ref, tile)

    def begin(sample, ref):
        for strip in range(strips):
            at = slice(strip * LANES, (strip + 1) * LANES)
            ref[strip, HALO : 2 * HALO] = above_ref[sample, :, at].astype(jnp.float32)
            ref[strip, 2 * HALO : 2 * HALO + rows] = flux_ref[sample, :, at].astype(jnp.float32)
            ref[strip, 2 * HALO + rows : HALO + tall] = below_ref[sample, :, at].astype(jnp.float32)

    def evolve(side, carry):
        sample = 2 * pair + side
        even = even_ref.at[side]
        count = jnp.minimum(steps_ref[sample], ITERS)
        half = lax.div(count, 2)

        @pl.when(lax.rem(count, 2) == 1)
        def _():
            begin(sample, odd_ref)
            step(odd_ref, even, half == 0)

        @pl.when(lax.rem(count, 2) == 0)
        def _():
            begin(sample, even)

        def two(k, carry):
            step(even, odd_ref, False)
            step(odd_ref, even, k == half - 1)
            return carry

        lax.fori_loop(0, half, two, 0)
        return carry

    lax.fori_loop(0, 2, evolve, 0)

    for turn, out_ref in enumerate((out0_ref, out1_ref, out2_ref, out3_ref)):
        low = pl.multiple_of(2 * HALO + 8 * lax.rem(own + turn, PARTS), 8)
        for strip in range(strips):
            both = [even_ref[side, strip, pl.ds(low, 8)] for side in range(2)]
            out_ref[:, strip * LANES : (strip + 1) * LANES] = jnp.concatenate(both, axis=0).astype(jnp.bfloat16)


def dots_kernel(own_ref, loc_ref, prints_ref, *refs):
    parts = refs[: PARTS * 2]
    out_ref, sums_ref = refs[PARTS * 2 :]
    peers, _, width = prints_ref.shape
    slots = peers * CAP
    prints = prints_ref[...].reshape(slots * 8, width)
    for low in range(0, TILES_DEV, 2):
        tiles = range(low, min(low + 2, TILES_DEV))
        cells = jnp.concatenate(
            [part[:, tile * width : (tile + 1) * width] for tile in tiles for part in parts], axis=0
        )
        sums = lax.dot_general(prints, cells, (((1,), (1,)), ((), ())), preferred_element_type=jnp.float32)
        for i, tile in enumerate(tiles):
            sums_ref[tile] = sums[:, i * LANES : (i + 1) * LANES].reshape(slots, 8, LANES)
    same = lax.rem(lax.broadcasted_iota(jnp.int32, (8, LANES), 1), 8) == lax.broadcasted_iota(
        jnp.int32, (8, LANES), 0
    )
    shift = 32 * own_ref[0]

    def pick(group, carry):
        at = pl.multiple_of(group * 8, 8)
        rows = [
            jnp.sum(jnp.where(same, sums_ref[loc_ref[at + i], at + i], 0.0), axis=0, keepdims=True) for i in range(8)
        ]
        out_ref[pl.ds(at, 8)] = pltpu.roll(jnp.concatenate(rows, axis=0), shift, 1)
        return carry

    lax.fori_loop(0, slots // 8, pick, 0, unroll=2)


def station_kernel(place_ref, count_ref, back_ref, out_ref, sums_ref):
    stations = sums_ref.shape[0]
    for station in range(stations):
        total = back_ref[pl.ds(place_ref[KT * station], 1)]
        for k in range(1, KT):
            row = back_ref[pl.ds(place_ref[KT * station + k], 1)]
            total = total + jnp.where(k < count_ref[station], row, 0.0)
        sums_ref[station : station + 1] = jnp.where(0 < count_ref[station], total, 0.0)
    lane = lax.broadcasted_iota(jnp.int32, (LANES, 16), 0)
    sample = lax.broadcasted_iota(jnp.int32, (LANES, 16), 1)
    fold = (lax.div(lane, 8) == sample).astype(jnp.float32)
    out_ref[...] = jnp.dot(
        sums_ref[...], fold, precision=lax.Precision.HIGHEST, preferred_element_type=jnp.float32
    )


def body(flux, coeff, diff_steps, footprint, tile_src, tile_local, tile_count):
    samples, rows, lon = flux.shape
    stations = footprint.shape[0]
    slots = stations * KT
    bands = lax.axis_size("station")
    band = lax.axis_index("station")
    part = lax.axis_index("sample")
    own = part.astype(jnp.int32).reshape(1)
    cells = rows * TILE_LON // PARTS
    down = [(i, i + 1) for i in range(bands - 1)]
    up = [(i + 1, i) for i in range(bands - 1)]

    last, first = pl.pallas_call(
        edge_kernel,
        out_shape=[jax.ShapeDtypeStruct((samples + 2, HALO, lon), jnp.bfloat16)] * 2,
        in_specs=[spec(VMEM)] * 2,
        out_specs=[spec(VMEM)] * 2,
        name="edges",
    )(flux, coeff)
    above = lax.ppermute(last, "station", down)
    below = lax.ppermute(first, "station", up)

    src_all = tile_src[:, :, 0].T
    my_src = lax.dynamic_slice_in_dim(src_all, band * stations, stations, axis=1)
    sent, place = pl.pallas_call(
        pack_kernel,
        out_shape=(
            jax.ShapeDtypeStruct((bands, 8 * CAP, TILE_LON), jnp.bfloat16),
            jax.ShapeDtypeStruct((slots,), jnp.int32),
        ),
        grid_spec=pltpu.PrefetchScalarGridSpec(
            num_scalar_prefetch=2,
            grid=(1,),
            in_specs=[pl.BlockSpec((stations, KT, cells), lambda i, part, src: (0, 0, part[0]))],
            out_specs=(
                pl.BlockSpec((bands, 8 * CAP, TILE_LON), lambda i, part, src: (0, 0, 0)),
                spec(SMEM),
            ),
            scratch_shapes=[
                SMEM((bands,), jnp.int32),
                SMEM((CAP * bands,), jnp.int32),
                VMEM((bands, 8 * CAP, 8 * slots), jnp.bfloat16),
            ],
        ),
        compiler_params=pltpu.CompilerParams(vmem_limit_bytes=24 * 2**20),
        name="pack",
    )(own, my_src, footprint)
    sent, _, _ = lax.optimization_barrier((sent, above, below))
    arrived = lax.all_to_all(sent, "station", split_axis=0, concat_axis=0, tiled=True)

    parts = [None] * (2 * PARTS)
    for pair in range(samples // 2):
        finals = pl.pallas_call(
            functools.partial(diffuse_kernel, pair),
            out_shape=[jax.ShapeDtypeStruct((16, lon), jnp.bfloat16)] * PARTS,
            in_specs=[spec(SMEM), spec(SMEM)] + [spec(VMEM)] * 4,
            out_specs=[spec(VMEM)] * PARTS,
            scratch_shapes=[
                VMEM((2, lon // LANES, rows + 4 * HALO, LANES), jnp.float32),
                VMEM((lon // LANES, rows + 4 * HALO, LANES), jnp.float32),
                VMEM((lon // LANES, rows + 2 * HALO, LANES), jnp.float32),
            ],
            compiler_params=pltpu.CompilerParams(vmem_limit_bytes=24 * 2**20),
            name="diffuse",
        )(own, diff_steps, flux, above, below, coeff)
        for j in range(PARTS):
            turn = (PARTS - j) % PARTS
            parts[2 * j + pair] = finals[0]
            if turn:
                parts[2 * j + pair] = lax.ppermute(
                    finals[turn], "sample", [(i, (i + turn) % PARTS) for i in range(PARTS)]
                )

    order = jnp.arange(stations * bands, dtype=jnp.int32) % stations
    code = (order[None, :] * KT + jnp.arange(KT, dtype=jnp.int32)[:, None]) * 8 + tile_local.T
    named = src_all == band
    first = jnp.min(jnp.min(jnp.where(named, code, slots * 8), axis=0).reshape(bands, stations), axis=1)
    last = jnp.max(jnp.max(jnp.where(named, code, 0), axis=0).reshape(bands, stations), axis=1)
    loc = jnp.stack([first & 7, last & 7], axis=1)

    values = pl.pallas_call(
        dots_kernel,
        out_shape=jax.ShapeDtypeStruct((bands * CAP, LANES), jnp.float32),
        in_specs=[spec(SMEM)] * 2 + [spec(VMEM)] * (1 + 2 * PARTS),
        out_specs=spec(VMEM),
        scratch_shapes=[VMEM((TILES_DEV, bands * CAP, 8, LANES), jnp.float32)],
        compiler_params=pltpu.CompilerParams(vmem_limit_bytes=24 * 2**20),
        name="dots",
    )(own, loc.reshape(-1), arrived, *parts)

    back = lax.all_to_all(values.reshape(bands, CAP, LANES), "station", split_axis=0, concat_axis=0, tiled=True)
    share = pl.pallas_call(
        station_kernel,
        out_shape=jax.ShapeDtypeStruct((stations, 16), jnp.float32),
        in_specs=[spec(SMEM), spec(SMEM), spec(VMEM)],
        out_specs=spec(VMEM),
        scratch_shapes=[VMEM((stations, LANES), jnp.float32)],
        name="stations",
    )(place, tile_count, back.reshape(bands * CAP, LANES))
    others = [lax.ppermute(share, "sample", [(i, i ^ flip) for i in range(PARTS)]) for flip in (1, 2, 3)]
    return (share + others[0]) + (others[1] + others[2])


def solution(mesh):
    in_specs = (
        P("sample", "station", None),
        P("station", None),
        P("sample"),
        P("station", None, None),
        P(),
        P(),
        P("station"),
    )
    return jax.shard_map(body, mesh=mesh, in_specs=in_specs, out_specs=P("station", None), check_vma=False)
```

```python
import jax
import jax.numpy as jnp
from jax import lax
from jax.experimental import pallas as pl
from jax.experimental.pallas import tpu as pltpu
from jax.sharding import PartitionSpec as P

TILE_LON = 512
TILES_DEV = 7
KT = 4
ITERS = 6
CAP = 2
HALO = 8
PARTS = 4
LANES = 128
VMEM = pltpu.VMEM
SMEM = pltpu.SMEM
HBM = pltpu.HBM


def spec(space):
    return pl.BlockSpec(memory_space=space)


def pack_kernel(
    part_ref, band_ref, src_hbm, prints_hbm, sent_hbm, place_ref,
    src_ref, held_ref, slot_ref, prints_ref, hot_ref, sent_ref, sems,
):
    bands, _, width = sent_ref.shape
    stations, _, cells = prints_ref.shape
    slots = stations * KT
    low = pl.multiple_of(part_ref[0] * cells, cells)
    prints_in = pltpu.make_async_copy(prints_hbm.at[:, :, pl.ds(low, cells)], prints_ref, sems.at[0])
    prints_in.start()
    first = band_ref[0] * stations
    low = pl.multiple_of(lax.div(first, LANES) * LANES, LANES)
    src_in = pltpu.make_async_copy(src_hbm.at[:, :, pl.ds(low, LANES)], src_ref, sems.at[1])
    src_in.start()
    first = lax.rem(first, LANES)

    def clear(i, carry):
        held_ref[i] = 0
        for rank in range(CAP):
            slot_ref[CAP * i + rank] = -(1 << 20)
        return carry

    lax.fori_loop(0, bands, clear, 0, unroll=8)
    src_in.wait()

    def assign(station, carry):
        for k in range(KT):
            band = src_ref[k, 0, first + station]
            rank = jnp.minimum(held_ref[band], CAP - 1)
            held_ref[band] = rank + 1
            place_ref[KT * station + k] = CAP * band + rank
            slot_ref[CAP * band + rank] = KT * station + k
        return carry

    lax.fori_loop(0, stations, assign, 0)

    row = lax.broadcasted_iota(jnp.int32, (8, width), 0)
    offset = lax.broadcasted_iota(jnp.int32, (8, width), 1) - slots * row

    def heat(i, carry):
        rows = [jnp.where(offset == slot_ref[CAP * i + rank], 1.0, 0.0) for rank in range(CAP)]
        hot_ref[i] = jnp.concatenate(rows, axis=0).astype(jnp.bfloat16)
        return carry

    lax.fori_loop(0, bands, heat, 0, unroll=8)

    prints_in.wait()
    flat = prints_ref[...].reshape(slots, cells)
    stacked = jnp.concatenate([flat[:, r * width : (r + 1) * width] for r in range(8)], axis=0)
    some = bands // 4
    copies = []
    for turn in range(4):
        at = slice(turn * some, (turn + 1) * some)
        hot = hot_ref[at].reshape(some * 16, slots * 8)
        moved = jnp.dot(hot, stacked, preferred_element_type=jnp.float32).astype(jnp.bfloat16)
        sent_ref[at] = moved.reshape(some, 16, width)
        copies.append(pltpu.make_async_copy(sent_ref.at[at], sent_hbm.at[at], sems.at[2 + turn]))
        copies[-1].start()
    for copy in copies:
        copy.wait()


def edge_kernel(flux_ref, coef_ref, last_ref, first_ref):
    samples, rows, _ = flux_ref.shape
    for ref, low in ((last_ref, rows - HALO), (first_ref, 0)):
        ref[0:samples] = flux_ref[:, low : low + HALO]
        coef = coef_ref[low : low + HALO]
        head = coef.astype(jnp.bfloat16)
        ref[samples] = head
        ref[samples + 1] = (coef - head.astype(jnp.float32)).astype(jnp.bfloat16)


def diffuse_kernel(
    own_ref, steps_ref, flux_ref, above_ref, below_ref, coef_ref,
    out0_hbm, out1_hbm, out2_hbm, out3_hbm, even_ref, odd_ref, coefs_ref, out_ref, sems,
):
    own = own_ref[0]
    samples, rows, lon = flux_ref.shape
    strips = lon // LANES
    tall = rows + 2 * HALO
    edge = jnp.zeros((HALO, LANES), jnp.float32)
    lane = lax.broadcasted_iota(jnp.int32, (8, LANES), 1)
    first_lane = lane == 0
    last_lane = lane == LANES - 1

    for strip in range(strips):
        at = slice(strip * LANES, (strip + 1) * LANES)
        for ref, low in ((above_ref, 0), (below_ref, HALO + rows)):
            coefs_ref[strip, low : low + HALO] = ref[samples, :, at].astype(jnp.float32) + ref[
                samples + 1, :, at
            ].astype(jnp.float32)
        coefs_ref[strip, HALO : HALO + rows] = coef_ref[:, at]
        for low in (0, HALO + tall):
            odd_ref[strip, low : low + HALO] = edge
            for sample in range(samples):
                even_ref[sample, strip, low : low + HALO] = edge

    def update(old_ref, new_ref, tile):
        at = HALO + 8 * tile

        def load(strip):
            return old_ref[strip % strips, at : at + 8]

        before = pltpu.roll(load(strips - 1), 1, 1)
        center = load(0)
        ahead = pltpu.roll(center, LANES - 1, 1)
        for strip in range(strips):
            behind = pltpu.roll(center, 1, 1)
            following = load(strip + 1)
            after = pltpu.roll(following, LANES - 1, 1)
            west = jnp.where(first_lane, before, behind)
            east = jnp.where(last_lane, after, ahead)
            north = old_ref[strip, at - 1 : at + 7]
            south = old_ref[strip, at + 1 : at + 9]
            lap = (north + south + east + west) - 4.0 * center
            new_ref[strip, at : at + 8] = center + coefs_ref[strip, 8 * tile : 8 * tile + 8] * lap
            before, center, ahead = behind, following, after

    def step(old_ref, new_ref, last):
        @pl.when(jnp.logical_not(last))
        def _():
            update(old_ref, new_ref, 0)
            update(old_ref, new_ref, tall // 8 - 1)

        for tile in range(1, tall // 8 - 1):
            update(old_ref, new_ref, tile)

    def begin(sample, ref):
        for strip in range(strips):
            at = slice(strip * LANES, (strip + 1) * LANES)
            ref[strip, HALO : 2 * HALO] = above_ref[sample, :, at].astype(jnp.float32)
            ref[strip, 2 * HALO : 2 * HALO + rows] = flux_ref[sample, :, at].astype(jnp.float32)
            ref[strip, 2 * HALO + rows : HALO + tall] = below_ref[sample, :, at].astype(jnp.float32)

    def evolve(sample, carry):
        even = even_ref.at[sample]
        count = jnp.minimum(steps_ref[sample], ITERS)
        half = lax.div(count, 2)

        @pl.when(lax.rem(count, 2) == 1)
        def _():
            begin(sample, odd_ref)
            step(odd_ref, even, half == 0)

        @pl.when(lax.rem(count, 2) == 0)
        def _():
            begin(sample, even)

        def two(k, carry):
            step(even, odd_ref, False)
            step(odd_ref, even, k == half - 1)
            return carry

        lax.fori_loop(0, half, two, 0)
        return carry

    lax.fori_loop(0, samples, evolve, 0)

    copies = []
    for turn, out_hbm in ((2, out2_hbm), (1, out1_hbm), (3, out3_hbm), (0, out0_hbm)):
        low = pl.multiple_of(2 * HALO + 8 * lax.rem(own + turn, PARTS), 8)
        for pair in range(samples // 2):
            for strip in range(strips):
                both = [even_ref[2 * pair + side, strip, pl.ds(low, 8)] for side in range(2)]
                out_ref[turn, 16 * pair : 16 * pair + 16, strip * LANES : (strip + 1) * LANES] = jnp.concatenate(
                    both, axis=0
                ).astype(jnp.bfloat16)
        copies.append(pltpu.make_async_copy(out_ref.at[turn], out_hbm, sems.at[turn]))
        copies[-1].start()
    for copy in copies:
        copy.wait()


def dots_kernel(own_ref, loc_ref, prints_ref, *refs):
    parts = refs[:PARTS]
    out_ref, sums_ref = refs[PARTS:]
    bands, _, width = prints_ref.shape
    slots = bands * CAP
    prints = prints_ref[...].reshape(slots * 8, width)
    for low in range(0, TILES_DEV, 2):
        tiles = range(low, min(low + 2, TILES_DEV))
        cells = jnp.concatenate(
            [part[:, tile * width : (tile + 1) * width] for tile in tiles for part in parts], axis=0
        )
        sums = lax.dot_general(prints, cells, (((1,), (1,)), ((), ())), preferred_element_type=jnp.float32)
        for i, tile in enumerate(tiles):
            sums_ref[tile] = sums[:, i * LANES : (i + 1) * LANES].reshape(slots, 8, LANES)
    same = lax.rem(lax.broadcasted_iota(jnp.int32, (8, LANES), 1), 8) == lax.broadcasted_iota(
        jnp.int32, (8, LANES), 0
    )
    shift = 32 * own_ref[0]

    def pick(group, carry):
        at = pl.multiple_of(group * 8, 8)
        rows = [
            jnp.sum(jnp.where(same, sums_ref[loc_ref[at + i], at + i], 0.0), axis=0, keepdims=True) for i in range(8)
        ]
        out_ref[pl.ds(at, 8)] = pltpu.roll(jnp.concatenate(rows, axis=0), shift, 1)
        return carry

    lax.fori_loop(0, slots // 8, pick, 0, unroll=2)


def station_kernel(place_ref, count_ref, back_ref, out_ref, sums_ref):
    stations = sums_ref.shape[0]
    for station in range(stations):
        total = back_ref[pl.ds(place_ref[KT * station], 1)]
        for k in range(1, KT):
            row = back_ref[pl.ds(place_ref[KT * station + k], 1)]
            total = total + jnp.where(k < count_ref[station], row, 0.0)
        sums_ref[station : station + 1] = jnp.where(0 < count_ref[station], total, 0.0)
    lane = lax.broadcasted_iota(jnp.int32, (LANES, 16), 0)
    sample = lax.broadcasted_iota(jnp.int32, (LANES, 16), 1)
    fold = (lax.div(lane, 8) == sample).astype(jnp.float32)
    out_ref[...] = jnp.dot(
        sums_ref[...], fold, precision=lax.Precision.HIGHEST, preferred_element_type=jnp.float32
    )


def body(flux, coeff, diff_steps, footprint, tile_src, tile_local, tile_count):
    samples, rows, lon = flux.shape
    stations = footprint.shape[0]
    slots = stations * KT
    bands = lax.axis_size("station")
    band = lax.axis_index("station")
    part = lax.axis_index("sample")
    own = part.astype(jnp.int32).reshape(1)
    cells = rows * TILE_LON // PARTS
    down = [(i, i + 1) for i in range(bands - 1)]
    up = [(i + 1, i) for i in range(bands - 1)]

    last, first = pl.pallas_call(
        edge_kernel,
        out_shape=[jax.ShapeDtypeStruct((samples + 2, HALO, lon), jnp.bfloat16)] * 2,
        in_specs=[spec(VMEM)] * 2,
        out_specs=[spec(VMEM)] * 2,
        name="edges",
    )(flux, coeff)
    above = lax.ppermute(last, "station", down)
    below = lax.ppermute(first, "station", up)

    src_all = tile_src[:, :, 0].T
    sent, place = pl.pallas_call(
        pack_kernel,
        out_shape=(
            jax.ShapeDtypeStruct((bands, 8 * CAP, TILE_LON), jnp.bfloat16),
            jax.ShapeDtypeStruct((slots,), jnp.int32),
        ),
        in_specs=[spec(SMEM), spec(SMEM), spec(HBM), spec(HBM)],
        out_specs=(spec(HBM), spec(SMEM)),
        scratch_shapes=[
            SMEM((KT, 1, LANES), jnp.int32),
            SMEM((bands,), jnp.int32),
            SMEM((CAP * bands,), jnp.int32),
            VMEM((stations, KT, cells), jnp.bfloat16),
            VMEM((bands, 8 * CAP, 8 * slots), jnp.bfloat16),
            VMEM((bands, 8 * CAP, TILE_LON), jnp.bfloat16),
            pltpu.SemaphoreType.DMA((6,)),
        ],
        compiler_params=pltpu.CompilerParams(vmem_limit_bytes=24 * 2**20),
        name="pack",
    )(own, band.astype(jnp.int32).reshape(1), tile_src.transpose(1, 2, 0), footprint)
    sent, _, _ = lax.optimization_barrier((sent, above, below))
    arrived = lax.all_to_all(sent, "station", split_axis=0, concat_axis=0, tiled=True)

    finals = pl.pallas_call(
        diffuse_kernel,
        out_shape=[jax.ShapeDtypeStruct((samples * 8, lon), jnp.bfloat16)] * PARTS,
        in_specs=[spec(SMEM), spec(SMEM)] + [spec(VMEM)] * 4,
        out_specs=[spec(HBM)] * PARTS,
        scratch_shapes=[
            VMEM((samples, lon // LANES, rows + 4 * HALO, LANES), jnp.float32),
            VMEM((lon // LANES, rows + 4 * HALO, LANES), jnp.float32),
            VMEM((lon // LANES, rows + 2 * HALO, LANES), jnp.float32),
            VMEM((PARTS, samples * 8, lon), jnp.bfloat16),
            pltpu.SemaphoreType.DMA((PARTS,)),
        ],
        compiler_params=pltpu.CompilerParams(vmem_limit_bytes=24 * 2**20),
        name="diffuse",
    )(own, diff_steps, flux, above, below, coeff)
    parts = [finals[0]] + [
        lax.ppermute(finals[turn], "sample", [(i, (i + turn) % PARTS) for i in range(PARTS)]) for turn in (3, 2, 1)
    ]

    order = jnp.arange(stations * bands, dtype=jnp.int32) % stations
    code = (order[None, :] * KT + jnp.arange(KT, dtype=jnp.int32)[:, None]) * 8 + tile_local.T
    named = src_all == band
    first = jnp.min(jnp.min(jnp.where(named, code, slots * 8), axis=0).reshape(bands, stations), axis=1)
    last = jnp.max(jnp.max(jnp.where(named, code, 0), axis=0).reshape(bands, stations), axis=1)
    loc = jnp.stack([first & 7, last & 7], axis=1)

    values = pl.pallas_call(
        dots_kernel,
        out_shape=jax.ShapeDtypeStruct((bands * CAP, LANES), jnp.float32),
        in_specs=[spec(SMEM)] * 2 + [spec(VMEM)] * (1 + PARTS),
        out_specs=spec(VMEM),
        scratch_shapes=[VMEM((TILES_DEV, bands * CAP, 8, LANES), jnp.float32)],
        compiler_params=pltpu.CompilerParams(vmem_limit_bytes=24 * 2**20),
        name="dots",
    )(own, loc.reshape(-1), arrived, *parts)

    back = lax.all_to_all(values.reshape(bands, CAP, LANES), "station", split_axis=0, concat_axis=0, tiled=True)
    share = pl.pallas_call(
        station_kernel,
        out_shape=jax.ShapeDtypeStruct((stations, 16), jnp.float32),
        in_specs=[spec(SMEM), spec(SMEM), spec(VMEM)],
        out_specs=spec(VMEM),
        scratch_shapes=[VMEM((stations, LANES), jnp.float32)],
        name="stations",
    )(place, tile_count, back.reshape(bands * CAP, LANES))
    others = [lax.ppermute(share, "sample", [(i, i ^ flip) for i in range(PARTS)]) for flip in (1, 2, 3)]
    return (share + others[0]) + (others[1] + others[2])


def solution(mesh):
    in_specs = (
        P("sample", "station", None),
        P("station", None),
        P("sample"),
        P("station", None, None),
        P(),
        P(),
        P("station"),
    )
    return jax.shard_map(body, mesh=mesh, in_specs=in_specs, out_specs=P("station", None), check_vma=False)
```

```python
import jax
import jax.numpy as jnp
from jax import lax
from jax.experimental import pallas as pl
from jax.experimental.pallas import tpu as pltpu
from jax.sharding import PartitionSpec as P

TILE_LON = 512
TILES_DEV = 7
KT = 4
ITERS = 6
CAP = 2
HALO = 8
PARTS = 4
LANES = 128
VMEM = pltpu.VMEM
SMEM = pltpu.SMEM
HBM = pltpu.HBM


def spec(space):
    return pl.BlockSpec(memory_space=space)


def pack_kernel(
    part_ref, band_ref, src_hbm, prints_hbm, sent_hbm, place_ref,
    src_ref, held_ref, slot_ref, prints_ref, hot_ref, sent_ref, sems,
):
    bands, _, width = sent_ref.shape
    stations, _, cells = prints_ref.shape
    slots = stations * KT
    low = pl.multiple_of(part_ref[0] * cells, cells)
    prints_in = pltpu.make_async_copy(prints_hbm.at[:, :, pl.ds(low, cells)], prints_ref, sems.at[0])
    prints_in.start()
    first = band_ref[0] * stations
    low = pl.multiple_of(lax.div(first, LANES) * LANES, LANES)
    src_in = pltpu.make_async_copy(src_hbm.at[:, :, pl.ds(low, LANES)], src_ref, sems.at[1])
    src_in.start()
    first = lax.rem(first, LANES)

    def clear(i, carry):
        held_ref[i] = 0
        for rank in range(CAP):
            slot_ref[CAP * i + rank] = -(1 << 20)
        return carry

    lax.fori_loop(0, bands, clear, 0, unroll=8)
    src_in.wait()

    def assign(station, carry):
        for k in range(KT):
            band = src_ref[k, 0, first + station]
            rank = jnp.minimum(held_ref[band], CAP - 1)
            held_ref[band] = rank + 1
            place_ref[KT * station + k] = CAP * band + rank
            slot_ref[CAP * band + rank] = KT * station + k
        return carry

    lax.fori_loop(0, stations, assign, 0)

    row = lax.broadcasted_iota(jnp.int32, (8, width), 0)
    offset = lax.broadcasted_iota(jnp.int32, (8, width), 1) - slots * row

    def heat(i, carry):
        rows = [jnp.where(offset == slot_ref[CAP * i + rank], 1.0, 0.0) for rank in range(CAP)]
        hot_ref[i] = jnp.concatenate(rows, axis=0).astype(jnp.bfloat16)
        return carry

    lax.fori_loop(0, bands, heat, 0, unroll=8)

    prints_in.wait()
    flat = prints_ref[...].reshape(slots, cells)
    stacked = jnp.concatenate([flat[:, r * width : (r + 1) * width] for r in range(8)], axis=0)
    some = bands // 4
    copies = []
    for turn in range(4):
        at = slice(turn * some, (turn + 1) * some)
        hot = hot_ref[at].reshape(some * 16, slots * 8)
        moved = jnp.dot(hot, stacked, preferred_element_type=jnp.float32).astype(jnp.bfloat16)
        sent_ref[at] = moved.reshape(some, 16, width)
        copies.append(pltpu.make_async_copy(sent_ref.at[at], sent_hbm.at[at], sems.at[2 + turn]))
        copies[-1].start()
    for copy in copies:
        copy.wait()


def edge_kernel(core_ref, flux_ref, coef_ref, away_ref, beside_ref):
    samples, rows, _ = flux_ref.shape

    def fill(ref, low):
        ref[0:samples] = flux_ref[:, low : low + HALO]
        coef = coef_ref[low : low + HALO]
        head = coef.astype(jnp.bfloat16)
        ref[samples] = head
        ref[samples + 1] = (coef - head.astype(jnp.float32)).astype(jnp.bfloat16)

    @pl.when(core_ref[0] == 0)
    def _():
        fill(away_ref, 0)
        fill(beside_ref, rows - HALO)

    @pl.when(core_ref[0] == 1)
    def _():
        fill(away_ref, rows - HALO)
        fill(beside_ref, 0)


def diffuse_kernel(
    own_ref, core_ref, steps_ref, flux_ref, away_ref, beside_ref, coef_ref,
    out0_hbm, out1_hbm, out2_hbm, out3_hbm, even_ref, odd_ref, coefs_ref, out_ref, sems,
):
    own = own_ref[0]
    samples, rows, lon = flux_ref.shape
    strips = lon // LANES
    tall = rows + 2 * HALO
    edge = jnp.zeros((HALO, LANES), jnp.float32)
    away = pl.multiple_of(core_ref[0] * (HALO + rows), 8)
    near = pl.multiple_of((1 - core_ref[0]) * (HALO + rows), 8)
    lane = lax.broadcasted_iota(jnp.int32, (8, LANES), 1)
    first_lane = lane == 0
    last_lane = lane == LANES - 1

    for strip in range(strips):
        at = slice(strip * LANES, (strip + 1) * LANES)
        for ref, low in ((away_ref, away), (beside_ref, near)):
            coefs_ref[strip, pl.ds(low, HALO)] = ref[samples, :, at].astype(jnp.float32) + ref[
                samples + 1, :, at
            ].astype(jnp.float32)
        coefs_ref[strip, HALO : HALO + rows] = coef_ref[:, at]
        for low in (0, HALO + tall):
            odd_ref[strip, low : low + HALO] = edge
            for sample in range(samples):
                even_ref[sample, strip, low : low + HALO] = edge

    def update(old_ref, new_ref, tile):
        at = HALO + 8 * tile

        def load(strip):
            return old_ref[strip % strips, at : at + 8]

        before = pltpu.roll(load(strips - 1), 1, 1)
        center = load(0)
        ahead = pltpu.roll(center, LANES - 1, 1)
        for strip in range(strips):
            behind = pltpu.roll(center, 1, 1)
            following = load(strip + 1)
            after = pltpu.roll(following, LANES - 1, 1)
            west = jnp.where(first_lane, before, behind)
            east = jnp.where(last_lane, after, ahead)
            north = old_ref[strip, at - 1 : at + 7]
            south = old_ref[strip, at + 1 : at + 9]
            lap = (north + south + east + west) - 4.0 * center
            new_ref[strip, at : at + 8] = center + coefs_ref[strip, 8 * tile : 8 * tile + 8] * lap
            before, center, ahead = behind, following, after

    def step(old_ref, new_ref, last):
        @pl.when(jnp.logical_not(last))
        def _():
            update(old_ref, new_ref, 0)
            update(old_ref, new_ref, tall // 8 - 1)

        for tile in range(1, tall // 8 - 1):
            update(old_ref, new_ref, tile)

    def begin(sample, ref):
        for strip in range(strips):
            at = slice(strip * LANES, (strip + 1) * LANES)
            ref[strip, pl.ds(HALO + away, HALO)] = away_ref[sample, :, at].astype(jnp.float32)
            ref[strip, 2 * HALO : 2 * HALO + rows] = flux_ref[sample, :, at].astype(jnp.float32)
            ref[strip, pl.ds(HALO + near, HALO)] = beside_ref[sample, :, at].astype(jnp.float32)

    def evolve(sample, carry):
        even = even_ref.at[sample]
        count = jnp.minimum(steps_ref[sample], ITERS)
        half = lax.div(count, 2)

        @pl.when(lax.rem(count, 2) == 1)
        def _():
            begin(sample, odd_ref)
            step(odd_ref, even, half == 0)

        @pl.when(lax.rem(count, 2) == 0)
        def _():
            begin(sample, even)

        def two(k, carry):
            step(even, odd_ref, False)
            step(odd_ref, even, k == half - 1)
            return carry

        lax.fori_loop(0, half, two, 0)
        return carry

    lax.fori_loop(0, samples, evolve, 0)

    copies = []
    for turn, out_hbm in ((2, out2_hbm), (1, out1_hbm), (3, out3_hbm), (0, out0_hbm)):
        low = pl.multiple_of(2 * HALO + 8 * lax.rem(own + turn, PARTS), 8)
        for pair in range(samples // 2):
            for strip in range(strips):
                both = [even_ref[2 * pair + side, strip, pl.ds(low, 8)] for side in range(2)]
                out_ref[turn, 16 * pair : 16 * pair + 16, strip * LANES : (strip + 1) * LANES] = jnp.concatenate(
                    both, axis=0
                ).astype(jnp.bfloat16)
        copies.append(pltpu.make_async_copy(out_ref.at[turn], out_hbm, sems.at[turn]))
        copies[-1].start()
    for copy in copies:
        copy.wait()


def dots_kernel(own_ref, loc_ref, prints_ref, *refs):
    parts = refs[:PARTS]
    out_ref, sums_ref = refs[PARTS:]
    bands, _, width = prints_ref.shape
    slots = bands * CAP
    prints = prints_ref[...].reshape(slots * 8, width)
    for low in range(0, TILES_DEV, 2):
        tiles = range(low, min(low + 2, TILES_DEV))
        cells = jnp.concatenate(
            [part[:, tile * width : (tile + 1) * width] for tile in tiles for part in parts], axis=0
        )
        sums = lax.dot_general(prints, cells, (((1,), (1,)), ((), ())), preferred_element_type=jnp.float32)
        for i, tile in enumerate(tiles):
            sums_ref[tile] = sums[:, i * LANES : (i + 1) * LANES].reshape(slots, 8, LANES)
    same = lax.rem(lax.broadcasted_iota(jnp.int32, (8, LANES), 1), 8) == lax.broadcasted_iota(
        jnp.int32, (8, LANES), 0
    )
    shift = 32 * own_ref[0]

    def pick(group, carry):
        at = pl.multiple_of(group * 8, 8)
        rows = [
            jnp.sum(jnp.where(same, sums_ref[loc_ref[at + i], at + i], 0.0), axis=0, keepdims=True) for i in range(8)
        ]
        out_ref[pl.ds(at, 8)] = pltpu.roll(jnp.concatenate(rows, axis=0), shift, 1)
        return carry

    lax.fori_loop(0, slots // 8, pick, 0, unroll=2)


def station_kernel(place_ref, count_ref, back_ref, out_ref, sums_ref):
    stations = sums_ref.shape[0]
    for station in range(stations):
        total = back_ref[pl.ds(place_ref[KT * station], 1)]
        for k in range(1, KT):
            row = back_ref[pl.ds(place_ref[KT * station + k], 1)]
            total = total + jnp.where(k < count_ref[station], row, 0.0)
        sums_ref[station : station + 1] = jnp.where(0 < count_ref[station], total, 0.0)
    lane = lax.broadcasted_iota(jnp.int32, (LANES, 16), 0)
    sample = lax.broadcasted_iota(jnp.int32, (LANES, 16), 1)
    fold = (lax.div(lane, 8) == sample).astype(jnp.float32)
    out_ref[...] = jnp.dot(
        sums_ref[...], fold, precision=lax.Precision.HIGHEST, preferred_element_type=jnp.float32
    )


def body(flux, coeff, diff_steps, footprint, tile_src, tile_local, tile_count):
    samples, rows, lon = flux.shape
    stations = footprint.shape[0]
    slots = stations * KT
    bands = lax.axis_size("station")
    band = lax.axis_index("station")
    part = lax.axis_index("sample")
    own = part.astype(jnp.int32).reshape(1)
    cells = rows * TILE_LON // PARTS
    core = lax.rem(band, 2).astype(jnp.int32).reshape(1)
    across = [(i, i + 1) for i in range(1, bands - 1, 2)] + [(i, i - 1) for i in range(2, bands, 2)]
    within = [(i, i ^ 1) for i in range(bands)]

    away, beside = pl.pallas_call(
        edge_kernel,
        out_shape=[jax.ShapeDtypeStruct((samples + 2, HALO, lon), jnp.bfloat16)] * 2,
        in_specs=[spec(SMEM)] + [spec(VMEM)] * 2,
        out_specs=[spec(VMEM)] * 2,
        name="edges",
    )(core, flux, coeff)
    away = lax.ppermute(away, "station", across)
    beside = lax.ppermute(beside, "station", within)

    src_all = tile_src[:, :, 0].T
    sent, place = pl.pallas_call(
        pack_kernel,
        out_shape=(
            jax.ShapeDtypeStruct((bands, 8 * CAP, TILE_LON), jnp.bfloat16),
            jax.ShapeDtypeStruct((slots,), jnp.int32),
        ),
        in_specs=[spec(SMEM), spec(SMEM), spec(HBM), spec(HBM)],
        out_specs=(spec(HBM), spec(SMEM)),
        scratch_shapes=[
            SMEM((KT, 1, LANES), jnp.int32),
            SMEM((bands,), jnp.int32),
            SMEM((CAP * bands,), jnp.int32),
            VMEM((stations, KT, cells), jnp.bfloat16),
            VMEM((bands, 8 * CAP, 8 * slots), jnp.bfloat16),
            VMEM((bands, 8 * CAP, TILE_LON), jnp.bfloat16),
            pltpu.SemaphoreType.DMA((6,)),
        ],
        compiler_params=pltpu.CompilerParams(vmem_limit_bytes=24 * 2**20),
        name="pack",
    )(
        own,
        band.astype(jnp.int32).reshape(1),
        pltpu.with_memory_space_constraint(tile_src.transpose(1, 2, 0), HBM),
        pltpu.with_memory_space_constraint(footprint, HBM),
    )
    sent, _, _ = lax.optimization_barrier((sent, away, beside))
    arrived = lax.all_to_all(sent, "station", split_axis=0, concat_axis=0, tiled=True)

    finals = pl.pallas_call(
        diffuse_kernel,
        out_shape=[jax.ShapeDtypeStruct((samples * 8, lon), jnp.bfloat16)] * PARTS,
        in_specs=[spec(SMEM)] * 3 + [spec(VMEM)] * 4,
        out_specs=[spec(HBM)] * PARTS,
        scratch_shapes=[
            VMEM((samples, lon // LANES, rows + 4 * HALO, LANES), jnp.float32),
            VMEM((lon // LANES, rows + 4 * HALO, LANES), jnp.float32),
            VMEM((lon // LANES, rows + 2 * HALO, LANES), jnp.float32),
            VMEM((PARTS, samples * 8, lon), jnp.bfloat16),
            pltpu.SemaphoreType.DMA((PARTS,)),
        ],
        compiler_params=pltpu.CompilerParams(vmem_limit_bytes=24 * 2**20),
        name="diffuse",
    )(own, core, diff_steps, flux, away, beside, coeff)
    parts = [finals[0]] + [
        lax.ppermute(finals[turn], "sample", [(i, (i + turn) % PARTS) for i in range(PARTS)]) for turn in (3, 2, 1)
    ]

    order = jnp.arange(stations * bands, dtype=jnp.int32) % stations
    code = (order[None, :] * KT + jnp.arange(KT, dtype=jnp.int32)[:, None]) * 8 + tile_local.T
    named = src_all == band
    first = jnp.min(jnp.min(jnp.where(named, code, slots * 8), axis=0).reshape(bands, stations), axis=1)
    last = jnp.max(jnp.max(jnp.where(named, code, 0), axis=0).reshape(bands, stations), axis=1)
    loc = jnp.stack([first & 7, last & 7], axis=1)

    values = pl.pallas_call(
        dots_kernel,
        out_shape=jax.ShapeDtypeStruct((bands * CAP, LANES), jnp.float32),
        in_specs=[spec(SMEM)] * 2 + [spec(VMEM)] * (1 + PARTS),
        out_specs=spec(VMEM),
        scratch_shapes=[VMEM((TILES_DEV, bands * CAP, 8, LANES), jnp.float32)],
        compiler_params=pltpu.CompilerParams(vmem_limit_bytes=24 * 2**20),
        name="dots",
    )(own, loc.reshape(-1), arrived, *parts)

    back = lax.all_to_all(values.reshape(bands, CAP, LANES), "station", split_axis=0, concat_axis=0, tiled=True)
    share = pl.pallas_call(
        station_kernel,
        out_shape=jax.ShapeDtypeStruct((stations, 16), jnp.float32),
        in_specs=[spec(SMEM), spec(SMEM), spec(VMEM)],
        out_specs=spec(VMEM),
        scratch_shapes=[VMEM((stations, LANES), jnp.float32)],
        name="stations",
    )(place, tile_count, back.reshape(bands * CAP, LANES))
    others = [lax.ppermute(share, "sample", [(i, i ^ flip) for i in range(PARTS)]) for flip in (1, 2, 3)]
    return (share + others[0]) + (others[1] + others[2])


def solution(mesh):
    in_specs = (
        P("sample", "station", None),
        P("station", None),
        P("sample"),
        P("station", None, None),
        P(),
        P(),
        P("station"),
    )
    return jax.shard_map(body, mesh=mesh, in_specs=in_specs, out_specs=P("station", None), check_vma=False)
```

```python
import jax
import jax.numpy as jnp
from jax import lax
from jax.experimental import pallas as pl
from jax.experimental.pallas import tpu as pltpu
from jax.sharding import PartitionSpec as P

TILE_LON = 512
TILES_DEV = 7
KT = 4
ITERS = 6
CAP = 2
HALO = 8
PARTS = 4
LANES = 128
VMEM = pltpu.VMEM
SMEM = pltpu.SMEM
HBM = pltpu.HBM


def spec(space):
    return pl.BlockSpec(memory_space=space)


def pack_kernel(
    src_hbm, prints_hbm, sent_hbm, place_ref,
    src_ref, held_ref, slot_ref, prints_ref, hot_ref, sent_ref, sems,
):
    bands, _, width = sent_ref.shape
    stations, _, cells = prints_ref.shape
    slots = stations * KT
    low = pl.multiple_of(lax.axis_index("sample") * cells, cells)
    prints_in = pltpu.make_async_copy(prints_hbm.at[:, :, pl.ds(low, cells)], prints_ref, sems.at[0])
    prints_in.start()
    first = lax.axis_index("station") * stations
    low = pl.multiple_of(lax.div(first, LANES) * LANES, LANES)
    src_in = pltpu.make_async_copy(src_hbm.at[:, :, pl.ds(low, LANES)], src_ref, sems.at[1])
    src_in.start()
    first = lax.rem(first, LANES)

    def clear(i, carry):
        held_ref[i] = 0
        for rank in range(CAP):
            slot_ref[CAP * i + rank] = -(1 << 20)
        return carry

    lax.fori_loop(0, bands, clear, 0, unroll=8)
    src_in.wait()

    def assign(station, carry):
        for k in range(KT):
            band = src_ref[k, 0, first + station]
            rank = jnp.minimum(held_ref[band], CAP - 1)
            held_ref[band] = rank + 1
            place_ref[KT * station + k] = CAP * band + rank
            slot_ref[CAP * band + rank] = KT * station + k
        return carry

    lax.fori_loop(0, stations, assign, 0)

    row = lax.broadcasted_iota(jnp.int32, (8, width), 0)
    offset = lax.broadcasted_iota(jnp.int32, (8, width), 1) - slots * row

    def heat(i, carry):
        rows = [jnp.where(offset == slot_ref[CAP * i + rank], 1.0, 0.0) for rank in range(CAP)]
        hot_ref[i] = jnp.concatenate(rows, axis=0).astype(jnp.bfloat16)
        return carry

    lax.fori_loop(0, bands, heat, 0, unroll=8)

    prints_in.wait()
    flat = prints_ref[...].reshape(slots, cells)
    stacked = jnp.concatenate([flat[:, r * width : (r + 1) * width] for r in range(8)], axis=0)
    some = bands // 4
    copies = []
    for turn in range(4):
        at = slice(turn * some, (turn + 1) * some)
        hot = hot_ref[at].reshape(some * 16, slots * 8)
        moved = jnp.dot(hot, stacked, preferred_element_type=jnp.float32).astype(jnp.bfloat16)
        sent_ref[at] = moved.reshape(some, 16, width)
        copies.append(pltpu.make_async_copy(sent_ref.at[at], sent_hbm.at[at], sems.at[2 + turn]))
        copies[-1].start()
    for copy in copies:
        copy.wait()


def edge_kernel(core_ref, flux_ref, coef_ref, away_ref, beside_ref):
    samples, rows, _ = flux_ref.shape

    def fill(ref, low):
        ref[0:samples] = flux_ref[:, low : low + HALO]
        coef = coef_ref[low : low + HALO]
        head = coef.astype(jnp.bfloat16)
        ref[samples] = head
        ref[samples + 1] = (coef - head.astype(jnp.float32)).astype(jnp.bfloat16)

    @pl.when(core_ref[0] == 0)
    def _():
        fill(away_ref, 0)
        fill(beside_ref, rows - HALO)

    @pl.when(core_ref[0] == 1)
    def _():
        fill(away_ref, rows - HALO)
        fill(beside_ref, 0)


def diffuse_kernel(
    own_ref, core_ref, steps_ref, flux_ref, away_ref, beside_ref, coef_ref,
    out0_hbm, out1_hbm, out2_hbm, out3_hbm, even_ref, odd_ref, coefs_ref, out_ref, sems,
):
    own = own_ref[0]
    samples, rows, lon = flux_ref.shape
    strips = lon // LANES
    tall = rows + 2 * HALO
    edge = jnp.zeros((HALO, LANES), jnp.float32)
    away = pl.multiple_of(core_ref[0] * (HALO + rows), 8)
    near = pl.multiple_of((1 - core_ref[0]) * (HALO + rows), 8)
    lane = lax.broadcasted_iota(jnp.int32, (8, LANES), 1)
    first_lane = lane == 0
    last_lane = lane == LANES - 1

    for strip in range(strips):
        at = slice(strip * LANES, (strip + 1) * LANES)
        for ref, low in ((away_ref, away), (beside_ref, near)):
            coefs_ref[strip, pl.ds(low, HALO)] = ref[samples, :, at].astype(jnp.float32) + ref[
                samples + 1, :, at
            ].astype(jnp.float32)
        coefs_ref[strip, HALO : HALO + rows] = coef_ref[:, at]
        for low in (0, HALO + tall):
            odd_ref[strip, low : low + HALO] = edge
            for sample in range(samples):
                even_ref[sample, strip, low : low + HALO] = edge

    def update(old_ref, new_ref, tile):
        at = HALO + 8 * tile

        def load(strip):
            return old_ref[strip % strips, at : at + 8]

        before = pltpu.roll(load(strips - 1), 1, 1)
        center = load(0)
        ahead = pltpu.roll(center, LANES - 1, 1)
        for strip in range(strips):
            behind = pltpu.roll(center, 1, 1)
            following = load(strip + 1)
            after = pltpu.roll(following, LANES - 1, 1)
            west = jnp.where(first_lane, before, behind)
            east = jnp.where(last_lane, after, ahead)
            north = old_ref[strip, at - 1 : at + 7]
            south = old_ref[strip, at + 1 : at + 9]
            lap = (north + south + east + west) - 4.0 * center
            new_ref[strip, at : at + 8] = center + coefs_ref[strip, 8 * tile : 8 * tile + 8] * lap
            before, center, ahead = behind, following, after

    def step(old_ref, new_ref, last):
        @pl.when(jnp.logical_not(last))
        def _():
            update(old_ref, new_ref, 0)
            update(old_ref, new_ref, tall // 8 - 1)

        for tile in range(1, tall // 8 - 1):
            update(old_ref, new_ref, tile)

    def begin(sample, ref):
        for strip in range(strips):
            at = slice(strip * LANES, (strip + 1) * LANES)
            ref[strip, pl.ds(HALO + away, HALO)] = away_ref[sample, :, at].astype(jnp.float32)
            ref[strip, 2 * HALO : 2 * HALO + rows] = flux_ref[sample, :, at].astype(jnp.float32)
            ref[strip, pl.ds(HALO + near, HALO)] = beside_ref[sample, :, at].astype(jnp.float32)

    def evolve(sample, carry):
        even = even_ref.at[sample]
        count = jnp.minimum(steps_ref[sample], ITERS)
        half = lax.div(count, 2)

        @pl.when(lax.rem(count, 2) == 1)
        def _():
            begin(sample, odd_ref)
            step(odd_ref, even, half == 0)

        @pl.when(lax.rem(count, 2) == 0)
        def _():
            begin(sample, even)

        def two(k, carry):
            step(even, odd_ref, False)
            step(odd_ref, even, k == half - 1)
            return carry

        lax.fori_loop(0, half, two, 0)
        return carry

    lax.fori_loop(0, samples, evolve, 0)

    copies = []
    for turn, out_hbm in ((2, out2_hbm), (1, out1_hbm), (3, out3_hbm), (0, out0_hbm)):
        low = pl.multiple_of(2 * HALO + 8 * lax.rem(own + turn, PARTS), 8)
        for pair in range(samples // 2):
            for strip in range(strips):
                both = [even_ref[2 * pair + side, strip, pl.ds(low, 8)] for side in range(2)]
                out_ref[turn, 16 * pair : 16 * pair + 16, strip * LANES : (strip + 1) * LANES] = jnp.concatenate(
                    both, axis=0
                ).astype(jnp.bfloat16)
        copies.append(pltpu.make_async_copy(out_ref.at[turn], out_hbm, sems.at[turn]))
        copies[-1].start()
    for copy in copies:
        copy.wait()


def dots_kernel(own_ref, loc_ref, prints_ref, *refs):
    parts = refs[:PARTS]
    out_ref, sums_ref = refs[PARTS:]
    bands, _, width = prints_ref.shape
    slots = bands * CAP
    prints = prints_ref[...].reshape(slots * 8, width)
    for low in range(0, TILES_DEV, 2):
        tiles = range(low, min(low + 2, TILES_DEV))
        cells = jnp.concatenate(
            [part[:, tile * width : (tile + 1) * width] for tile in tiles for part in parts], axis=0
        )
        sums = lax.dot_general(prints, cells, (((1,), (1,)), ((), ())), preferred_element_type=jnp.float32)
        for i, tile in enumerate(tiles):
            sums_ref[tile] = sums[:, i * LANES : (i + 1) * LANES].reshape(slots, 8, LANES)
    same = lax.rem(lax.broadcasted_iota(jnp.int32, (8, LANES), 1), 8) == lax.broadcasted_iota(
        jnp.int32, (8, LANES), 0
    )
    shift = 32 * own_ref[0]

    def pick(group, carry):
        at = pl.multiple_of(group * 8, 8)
        rows = [
            jnp.sum(jnp.where(same, sums_ref[loc_ref[at + i], at + i], 0.0), axis=0, keepdims=True) for i in range(8)
        ]
        out_ref[pl.ds(at, 8)] = pltpu.roll(jnp.concatenate(rows, axis=0), shift, 1)
        return carry

    lax.fori_loop(0, slots // 8, pick, 0, unroll=2)


def station_kernel(place_ref, count_ref, back_ref, out_ref, sums_ref):
    stations = sums_ref.shape[0]
    for station in range(stations):
        total = back_ref[pl.ds(place_ref[KT * station], 1)]
        for k in range(1, KT):
            row = back_ref[pl.ds(place_ref[KT * station + k], 1)]
            total = total + jnp.where(k < count_ref[station], row, 0.0)
        sums_ref[station : station + 1] = jnp.where(0 < count_ref[station], total, 0.0)
    lane = lax.broadcasted_iota(jnp.int32, (LANES, 16), 0)
    sample = lax.broadcasted_iota(jnp.int32, (LANES, 16), 1)
    fold = (lax.div(lane, 8) == sample).astype(jnp.float32)
    out_ref[...] = jnp.dot(
        sums_ref[...], fold, precision=lax.Precision.HIGHEST, preferred_element_type=jnp.float32
    )


def body(flux, coeff, diff_steps, footprint, tile_src, tile_local, tile_count):
    samples, rows, lon = flux.shape
    stations = footprint.shape[0]
    slots = stations * KT
    bands = lax.axis_size("station")
    band = lax.axis_index("station")
    part = lax.axis_index("sample")
    own = part.astype(jnp.int32).reshape(1)
    cells = rows * TILE_LON // PARTS
    core = lax.rem(band, 2).astype(jnp.int32).reshape(1)
    across = [(i, i + 1) for i in range(1, bands - 1, 2)] + [(i, i - 1) for i in range(2, bands, 2)]
    within = [(i, i ^ 1) for i in range(bands)]

    away, beside = pl.pallas_call(
        edge_kernel,
        out_shape=[jax.ShapeDtypeStruct((samples + 2, HALO, lon), jnp.bfloat16)] * 2,
        in_specs=[spec(SMEM)] + [spec(VMEM)] * 2,
        out_specs=[spec(VMEM)] * 2,
        name="edges",
    )(core, flux, coeff)
    away = lax.ppermute(away, "station", across)
    beside = lax.ppermute(beside, "station", within)

    src_all = tile_src[:, :, 0].T
    sent, place = pl.pallas_call(
        pack_kernel,
        out_shape=(
            HBM((bands, 8 * CAP, TILE_LON), jnp.bfloat16),
            HBM((slots,), jnp.int32),
        ),
        in_specs=[spec(HBM), spec(HBM)],
        out_specs=(spec(HBM), spec(SMEM)),
        scratch_shapes=[
            SMEM((KT, 1, LANES), jnp.int32),
            SMEM((bands,), jnp.int32),
            SMEM((CAP * bands,), jnp.int32),
            VMEM((stations, KT, cells), jnp.bfloat16),
            VMEM((bands, 8 * CAP, 8 * slots), jnp.bfloat16),
            VMEM((bands, 8 * CAP, TILE_LON), jnp.bfloat16),
            pltpu.SemaphoreType.DMA((6,)),
        ],
        compiler_params=pltpu.CompilerParams(vmem_limit_bytes=24 * 2**20),
        name="pack",
    )(
        pltpu.with_memory_space_constraint(tile_src.transpose(1, 2, 0), HBM),
        pltpu.with_memory_space_constraint(footprint, HBM),
    )
    sent, _, _ = lax.optimization_barrier((sent, away, beside))
    arrived = lax.all_to_all(sent, "station", split_axis=0, concat_axis=0, tiled=True)

    finals = pl.pallas_call(
        diffuse_kernel,
        out_shape=[HBM((samples * 8, lon), jnp.bfloat16)] * PARTS,
        in_specs=[spec(SMEM)] * 3 + [spec(VMEM)] * 4,
        out_specs=[spec(HBM)] * PARTS,
        scratch_shapes=[
            VMEM((samples, lon // LANES, rows + 4 * HALO, LANES), jnp.float32),
            VMEM((lon // LANES, rows + 4 * HALO, LANES), jnp.float32),
            VMEM((lon // LANES, rows + 2 * HALO, LANES), jnp.float32),
            VMEM((PARTS, samples * 8, lon), jnp.bfloat16),
            pltpu.SemaphoreType.DMA((PARTS,)),
        ],
        compiler_params=pltpu.CompilerParams(vmem_limit_bytes=24 * 2**20),
        name="diffuse",
    )(own, core, diff_steps, flux, away, beside, coeff)
    parts = [finals[0]] + [
        lax.ppermute(finals[turn], "sample", [(i, (i + turn) % PARTS) for i in range(PARTS)]) for turn in (3, 2, 1)
    ]

    local, _ = lax.optimization_barrier((tile_local, finals[0]))
    order = jnp.arange(stations * bands, dtype=jnp.int32) % stations
    code = (order[None, :] * KT + jnp.arange(KT, dtype=jnp.int32)[:, None]) * 8 + local.T
    named = src_all == band
    first = jnp.min(jnp.min(jnp.where(named, code, slots * 8), axis=0).reshape(bands, stations), axis=1)
    last = jnp.max(jnp.max(jnp.where(named, code, 0), axis=0).reshape(bands, stations), axis=1)
    loc = jnp.stack([first & 7, last & 7], axis=1)

    values = pl.pallas_call(
        dots_kernel,
        out_shape=jax.ShapeDtypeStruct((bands * CAP, LANES), jnp.float32),
        in_specs=[spec(SMEM)] * 2 + [spec(VMEM)] * (1 + PARTS),
        out_specs=spec(VMEM),
        scratch_shapes=[VMEM((TILES_DEV, bands * CAP, 8, LANES), jnp.float32)],
        compiler_params=pltpu.CompilerParams(vmem_limit_bytes=24 * 2**20),
        name="dots",
    )(own, loc.reshape(-1), arrived, *parts)

    back = lax.all_to_all(values.reshape(bands, CAP, LANES), "station", split_axis=0, concat_axis=0, tiled=True)
    share = pl.pallas_call(
        station_kernel,
        out_shape=jax.ShapeDtypeStruct((stations, 16), jnp.float32),
        in_specs=[spec(SMEM), spec(SMEM), spec(VMEM)],
        out_specs=spec(VMEM),
        scratch_shapes=[VMEM((stations, LANES), jnp.float32)],
        name="stations",
    )(place, tile_count, back.reshape(bands * CAP, LANES))
    others = [lax.ppermute(share, "sample", [(i, i ^ flip) for i in range(PARTS)]) for flip in (1, 2, 3)]
    return (share + others[0]) + (others[1] + others[2])


def solution(mesh):
    in_specs = (
        P("sample", "station", None),
        P("station", None),
        P("sample"),
        P("station", None, None),
        P(),
        P(),
        P("station"),
    )
    return jax.shard_map(body, mesh=mesh, in_specs=in_specs, out_specs=P("station", None), check_vma=False)
```

```python
import jax
import jax.numpy as jnp
from jax import lax
from jax.experimental import pallas as pl
from jax.experimental.pallas import tpu as pltpu
from jax.sharding import PartitionSpec as P

TILE_LON = 512
TILES_DEV = 7
KT = 4
ITERS = 6
CAP = 2
HALO = 8
PARTS = 4
LANES = 128
VMEM = pltpu.VMEM
SMEM = pltpu.SMEM
HBM = pltpu.HBM


def spec(space):
    return pl.BlockSpec(memory_space=space)


def pack_kernel(
    src_hbm, prints_hbm, sent_hbm, place_ref,
    src_ref, held_ref, slot_ref, prints_ref, hot_ref, sent_ref, sems,
):
    bands, _, width = sent_ref.shape
    stations, _, cells = prints_ref.shape
    slots = stations * KT
    low = pl.multiple_of(lax.axis_index("sample") * cells, cells)
    prints_in = pltpu.make_async_copy(prints_hbm.at[:, :, pl.ds(low, cells)], prints_ref, sems.at[0])
    prints_in.start()
    first = lax.axis_index("station") * stations
    low = pl.multiple_of(lax.div(first, LANES) * LANES, LANES)
    src_in = pltpu.make_async_copy(src_hbm.at[:, :, pl.ds(low, LANES)], src_ref, sems.at[1])
    src_in.start()
    first = lax.rem(first, LANES)

    def clear(i, carry):
        held_ref[i] = 0
        for rank in range(CAP):
            slot_ref[CAP * i + rank] = -(1 << 20)
        return carry

    lax.fori_loop(0, bands, clear, 0, unroll=8)
    src_in.wait()

    def assign(station, carry):
        for k in range(KT):
            band = src_ref[k, 0, first + station]
            rank = jnp.minimum(held_ref[band], CAP - 1)
            held_ref[band] = rank + 1
            place_ref[KT * station + k] = CAP * band + rank
            slot_ref[CAP * band + rank] = KT * station + k
        return carry

    lax.fori_loop(0, stations, assign, 0)

    row = lax.broadcasted_iota(jnp.int32, (8, width), 0)
    offset = lax.broadcasted_iota(jnp.int32, (8, width), 1) - slots * row

    def heat(i, carry):
        rows = [jnp.where(offset == slot_ref[CAP * i + rank], 1.0, 0.0) for rank in range(CAP)]
        hot_ref[i] = jnp.concatenate(rows, axis=0).astype(jnp.bfloat16)
        return carry

    lax.fori_loop(0, bands, heat, 0, unroll=8)

    prints_in.wait()
    flat = prints_ref[...].reshape(slots, cells)
    stacked = jnp.concatenate([flat[:, r * width : (r + 1) * width] for r in range(8)], axis=0)
    some = bands // 4
    copies = []
    for turn in range(4):
        at = slice(turn * some, (turn + 1) * some)
        hot = hot_ref[at].reshape(some * 16, slots * 8)
        moved = jnp.dot(hot, stacked, preferred_element_type=jnp.float32).astype(jnp.bfloat16)
        sent_ref[at] = moved.reshape(some, 16, width)
        copies.append(pltpu.make_async_copy(sent_ref.at[at], sent_hbm.at[at], sems.at[2 + turn]))
        copies[-1].start()
    for copy in copies:
        copy.wait()


def edge_kernel(core_ref, flux_ref, coef_ref, away_ref, beside_ref):
    samples, rows, _ = flux_ref.shape

    def fill(ref, low):
        ref[0:samples] = flux_ref[:, low : low + HALO]
        coef = coef_ref[low : low + HALO]
        head = coef.astype(jnp.bfloat16)
        ref[samples] = head
        ref[samples + 1] = (coef - head.astype(jnp.float32)).astype(jnp.bfloat16)

    @pl.when(core_ref[0] == 0)
    def _():
        fill(away_ref, 0)
        fill(beside_ref, rows - HALO)

    @pl.when(core_ref[0] == 1)
    def _():
        fill(away_ref, rows - HALO)
        fill(beside_ref, 0)


def diffuse_kernel(
    own_ref, core_ref, steps_ref, flux_ref, away_ref, beside_ref, coef_ref,
    out0_hbm, out1_hbm, out2_hbm, out3_hbm, even_ref, odd_ref, coefs_ref, out_ref, sems,
):
    own = own_ref[0]
    samples, rows, lon = flux_ref.shape
    strips = lon // LANES
    tall = rows + 2 * HALO
    edge = jnp.zeros((HALO, LANES), jnp.float32)
    away = pl.multiple_of(core_ref[0] * (HALO + rows), 8)
    near = pl.multiple_of((1 - core_ref[0]) * (HALO + rows), 8)
    lane = lax.broadcasted_iota(jnp.int32, (8, LANES), 1)
    first_lane = lane == 0
    last_lane = lane == LANES - 1

    for strip in range(strips):
        at = slice(strip * LANES, (strip + 1) * LANES)
        for ref, low in ((away_ref, away), (beside_ref, near)):
            coefs_ref[strip, pl.ds(low, HALO)] = ref[samples, :, at].astype(jnp.float32) + ref[
                samples + 1, :, at
            ].astype(jnp.float32)
        coefs_ref[strip, HALO : HALO + rows] = coef_ref[:, at]
        for low in (0, HALO + tall):
            odd_ref[strip, low : low + HALO] = edge
            for sample in range(samples):
                even_ref[sample, strip, low : low + HALO] = edge

    def update(old_ref, new_ref, tile):
        at = HALO + 8 * tile

        def load(strip):
            return old_ref[strip % strips, at : at + 8]

        before = pltpu.roll(load(strips - 1), 1, 1)
        center = load(0)
        ahead = pltpu.roll(center, LANES - 1, 1)
        for strip in range(strips):
            behind = pltpu.roll(center, 1, 1)
            following = load(strip + 1)
            after = pltpu.roll(following, LANES - 1, 1)
            west = jnp.where(first_lane, before, behind)
            east = jnp.where(last_lane, after, ahead)
            north = old_ref[strip, at - 1 : at + 7]
            south = old_ref[strip, at + 1 : at + 9]
            lap = (north + south + east + west) - 4.0 * center
            new_ref[strip, at : at + 8] = center + coefs_ref[strip, 8 * tile : 8 * tile + 8] * lap
            before, center, ahead = behind, following, after

    def step(old_ref, new_ref, last):
        @pl.when(jnp.logical_not(last))
        def _():
            update(old_ref, new_ref, 0)
            update(old_ref, new_ref, tall // 8 - 1)

        for tile in range(1, tall // 8 - 1):
            update(old_ref, new_ref, tile)

    def begin(sample, ref):
        for strip in range(strips):
            at = slice(strip * LANES, (strip + 1) * LANES)
            ref[strip, pl.ds(HALO + away, HALO)] = away_ref[sample, :, at].astype(jnp.float32)
            ref[strip, 2 * HALO : 2 * HALO + rows] = flux_ref[sample, :, at].astype(jnp.float32)
            ref[strip, pl.ds(HALO + near, HALO)] = beside_ref[sample, :, at].astype(jnp.float32)

    def evolve(sample, carry):
        even = even_ref.at[sample]
        count = jnp.minimum(steps_ref[sample], ITERS)
        half = lax.div(count, 2)

        @pl.when(lax.rem(count, 2) == 1)
        def _():
            begin(sample, odd_ref)
            step(odd_ref, even, half == 0)

        @pl.when(lax.rem(count, 2) == 0)
        def _():
            begin(sample, even)

        def two(k, carry):
            step(even, odd_ref, False)
            step(odd_ref, even, k == half - 1)
            return carry

        lax.fori_loop(0, half, two, 0)
        return carry

    lax.fori_loop(0, samples, evolve, 0)

    copies = []
    for turn, out_hbm in ((2, out2_hbm), (1, out1_hbm), (3, out3_hbm), (0, out0_hbm)):
        low = pl.multiple_of(2 * HALO + 8 * lax.rem(own + turn, PARTS), 8)
        for pair in range(samples // 2):
            for strip in range(strips):
                both = [even_ref[2 * pair + side, strip, pl.ds(low, 8)] for side in range(2)]
                out_ref[turn, 16 * pair : 16 * pair + 16, strip * LANES : (strip + 1) * LANES] = jnp.concatenate(
                    both, axis=0
                ).astype(jnp.bfloat16)
        copies.append(pltpu.make_async_copy(out_ref.at[turn], out_hbm, sems.at[turn]))
        copies[-1].start()
    for copy in copies:
        copy.wait()


def dots_kernel(own_ref, loc_ref, prints_ref, *refs):
    parts = refs[:PARTS]
    out_ref, sums_ref = refs[PARTS:]
    bands, _, width = prints_ref.shape
    slots = bands * CAP
    prints = prints_ref[...].reshape(slots * 8, width)
    for low in range(0, TILES_DEV, 2):
        tiles = range(low, min(low + 2, TILES_DEV))
        cells = jnp.concatenate(
            [part[:, tile * width : (tile + 1) * width] for tile in tiles for part in parts], axis=0
        )
        sums = lax.dot_general(prints, cells, (((1,), (1,)), ((), ())), preferred_element_type=jnp.float32)
        for i, tile in enumerate(tiles):
            sums_ref[tile] = sums[:, i * LANES : (i + 1) * LANES].reshape(slots, 8, LANES)
    same = lax.rem(lax.broadcasted_iota(jnp.int32, (8, LANES), 1), 8) == lax.broadcasted_iota(
        jnp.int32, (8, LANES), 0
    )
    shift = 32 * own_ref[0]

    def pick(group, carry):
        at = pl.multiple_of(group * 8, 8)
        rows = [
            jnp.sum(jnp.where(same, sums_ref[loc_ref[at + i], at + i], 0.0), axis=0, keepdims=True) for i in range(8)
        ]
        out_ref[pl.ds(at, 8)] = pltpu.roll(jnp.concatenate(rows, axis=0), shift, 1)
        return carry

    lax.fori_loop(0, slots // 8, pick, 0, unroll=2)


def station_kernel(place_ref, count_ref, back_ref, out_ref, sums_ref):
    stations = sums_ref.shape[0]
    for station in range(stations):
        total = back_ref[pl.ds(place_ref[KT * station], 1)]
        for k in range(1, KT):
            row = back_ref[pl.ds(place_ref[KT * station + k], 1)]
            total = total + jnp.where(k < count_ref[station], row, 0.0)
        sums_ref[station : station + 1] = jnp.where(0 < count_ref[station], total, 0.0)
    lane = lax.broadcasted_iota(jnp.int32, (LANES, 16), 0)
    sample = lax.broadcasted_iota(jnp.int32, (LANES, 16), 1)
    fold = (lax.div(lane, 8) == sample).astype(jnp.float32)
    out_ref[...] = jnp.dot(
        sums_ref[...], fold, precision=lax.Precision.HIGHEST, preferred_element_type=jnp.float32
    )


def body(flux, coeff, diff_steps, footprint, tile_src, tile_local, tile_count):
    samples, rows, lon = flux.shape
    stations = footprint.shape[0]
    slots = stations * KT
    bands = lax.axis_size("station")
    band = lax.axis_index("station")
    part = lax.axis_index("sample")
    own = part.astype(jnp.int32).reshape(1)
    cells = rows * TILE_LON // PARTS
    core = lax.rem(band, 2).astype(jnp.int32).reshape(1)
    across = [(i, i + 1) for i in range(1, bands - 1, 2)] + [(i, i - 1) for i in range(2, bands, 2)]
    within = [(i, i ^ 1) for i in range(bands)]

    away, beside = pl.pallas_call(
        edge_kernel,
        out_shape=[VMEM((samples + 2, HALO, lon), jnp.bfloat16)] * 2,
        in_specs=[spec(SMEM)] + [spec(VMEM)] * 2,
        out_specs=[spec(VMEM)] * 2,
        name="edges",
    )(core, flux, coeff)
    away = lax.ppermute(away, "station", across)
    beside = lax.ppermute(beside, "station", within)

    src_all = tile_src[:, :, 0].T
    sent, place = pl.pallas_call(
        pack_kernel,
        out_shape=(
            HBM((bands, 8 * CAP, TILE_LON), jnp.bfloat16),
            HBM((slots,), jnp.int32),
        ),
        in_specs=[spec(HBM), spec(HBM)],
        out_specs=(spec(HBM), spec(SMEM)),
        scratch_shapes=[
            SMEM((KT, 1, LANES), jnp.int32),
            SMEM((bands,), jnp.int32),
            SMEM((CAP * bands,), jnp.int32),
            VMEM((stations, KT, cells), jnp.bfloat16),
            VMEM((bands, 8 * CAP, 8 * slots), jnp.bfloat16),
            VMEM((bands, 8 * CAP, TILE_LON), jnp.bfloat16),
            pltpu.SemaphoreType.DMA((6,)),
        ],
        compiler_params=pltpu.CompilerParams(vmem_limit_bytes=24 * 2**20),
        name="pack",
    )(
        pltpu.with_memory_space_constraint(tile_src.transpose(1, 2, 0), HBM),
        pltpu.with_memory_space_constraint(footprint, HBM),
    )
    sent, _, _ = lax.optimization_barrier((sent, away, beside))
    arrived = lax.all_to_all(sent, "station", split_axis=0, concat_axis=0, tiled=True)

    finals = pl.pallas_call(
        diffuse_kernel,
        out_shape=[jax.ShapeDtypeStruct((samples * 8, lon), jnp.bfloat16)]
        + [HBM((samples * 8, lon), jnp.bfloat16)] * (PARTS - 1),
        in_specs=[spec(SMEM)] * 3 + [spec(VMEM)] * 4,
        out_specs=[spec(HBM)] * PARTS,
        scratch_shapes=[
            VMEM((samples, lon // LANES, rows + 4 * HALO, LANES), jnp.float32),
            VMEM((lon // LANES, rows + 4 * HALO, LANES), jnp.float32),
            VMEM((lon // LANES, rows + 2 * HALO, LANES), jnp.float32),
            VMEM((PARTS, samples * 8, lon), jnp.bfloat16),
            pltpu.SemaphoreType.DMA((PARTS,)),
        ],
        compiler_params=pltpu.CompilerParams(vmem_limit_bytes=24 * 2**20),
        name="diffuse",
    )(own, core, diff_steps, flux, away, beside, coeff)
    parts = [finals[0]] + [
        lax.ppermute(finals[turn], "sample", [(i, (i + turn) % PARTS) for i in range(PARTS)]) for turn in (3, 2, 1)
    ]

    local, _ = lax.optimization_barrier((tile_local, finals[0]))
    order = jnp.arange(stations * bands, dtype=jnp.int32) % stations
    code = (order[None, :] * KT + jnp.arange(KT, dtype=jnp.int32)[:, None]) * 8 + local.T
    named = src_all == band
    first = jnp.min(jnp.min(jnp.where(named, code, slots * 8), axis=0).reshape(bands, stations), axis=1)
    last = jnp.max(jnp.max(jnp.where(named, code, 0), axis=0).reshape(bands, stations), axis=1)
    loc = jnp.stack([first & 7, last & 7], axis=1)

    parts = [pltpu.with_memory_space_constraint(each, VMEM) for each in parts]
    values = pl.pallas_call(
        dots_kernel,
        out_shape=jax.ShapeDtypeStruct((bands * CAP, LANES), jnp.float32),
        in_specs=[spec(SMEM)] * 2 + [spec(VMEM)] * (1 + PARTS),
        out_specs=spec(VMEM),
        scratch_shapes=[VMEM((TILES_DEV, bands * CAP, 8, LANES), jnp.float32)],
        compiler_params=pltpu.CompilerParams(vmem_limit_bytes=24 * 2**20),
        name="dots",
    )(own, loc.reshape(-1), arrived, *parts)

    back = lax.all_to_all(values.reshape(bands, CAP, LANES), "station", split_axis=0, concat_axis=0, tiled=True)
    back = pltpu.with_memory_space_constraint(back.reshape(bands * CAP, LANES), VMEM)
    share = pl.pallas_call(
        station_kernel,
        out_shape=VMEM((stations, 16), jnp.float32),
        in_specs=[spec(SMEM), spec(SMEM), spec(VMEM)],
        out_specs=spec(VMEM),
        scratch_shapes=[VMEM((stations, LANES), jnp.float32)],
        name="stations",
    )(place, tile_count, back)
    others = [lax.ppermute(share, "sample", [(i, i ^ flip) for i in range(PARTS)]) for flip in (1, 2, 3)]
    return (share + others[0]) + (others[1] + others[2])


def solution(mesh):
    in_specs = (
        P("sample", "station", None),
        P("station", None),
        P("sample"),
        P("station", None, None),
        P(),
        P(),
        P("station"),
    )
    return jax.shard_map(body, mesh=mesh, in_specs=in_specs, out_specs=P("station", None), check_vma=False)
```

```python
import jax
import jax.numpy as jnp
from jax import lax
from jax.experimental import pallas as pl
from jax.experimental.pallas import tpu as pltpu
from jax.sharding import PartitionSpec as P

TILE_LON = 512
TILES_DEV = 7
KT = 4
ITERS = 6
CAP = 2
HALO = 8
PARTS = 4
LANES = 128
VMEM = pltpu.VMEM
SMEM = pltpu.SMEM
HBM = pltpu.HBM


def spec(space):
    return pl.BlockSpec(memory_space=space)


def pack_kernel(
    src_hbm, prints_hbm, sent_hbm, place_hbm,
    place_ref, src_ref, held_ref, slot_ref, prints_ref, hot_ref, sent_ref, sems,
):
    bands, _, width = sent_ref.shape
    stations, _, cells = prints_ref.shape
    slots = stations * KT
    low = pl.multiple_of(lax.axis_index("sample") * cells, cells)
    prints_in = pltpu.make_async_copy(prints_hbm.at[:, :, pl.ds(low, cells)], prints_ref, sems.at[0])
    prints_in.start()
    first = lax.axis_index("station") * stations
    low = pl.multiple_of(lax.div(first, LANES) * LANES, LANES)
    src_in = pltpu.make_async_copy(src_hbm.at[:, :, pl.ds(low, LANES)], src_ref, sems.at[1])
    src_in.start()
    first = lax.rem(first, LANES)

    def clear(i, carry):
        held_ref[i] = 0
        for rank in range(CAP):
            slot_ref[CAP * i + rank] = -(1 << 20)
        return carry

    lax.fori_loop(0, bands, clear, 0, unroll=8)
    src_in.wait()

    def assign(station, carry):
        for k in range(KT):
            band = src_ref[k, 0, first + station]
            rank = jnp.minimum(held_ref[band], CAP - 1)
            held_ref[band] = rank + 1
            place_ref[KT * station + k] = CAP * band + rank
            slot_ref[CAP * band + rank] = KT * station + k
        return carry

    lax.fori_loop(0, stations, assign, 0)
    copies = [pltpu.make_async_copy(place_ref, place_hbm, sems.at[6])]
    copies[0].start()

    row = lax.broadcasted_iota(jnp.int32, (8, width), 0)
    offset = lax.broadcasted_iota(jnp.int32, (8, width), 1) - slots * row

    def heat(i, carry):
        rows = [jnp.where(offset == slot_ref[CAP * i + rank], 1.0, 0.0) for rank in range(CAP)]
        hot_ref[i] = jnp.concatenate(rows, axis=0).astype(jnp.bfloat16)
        return carry

    lax.fori_loop(0, bands, heat, 0, unroll=8)

    prints_in.wait()
    flat = prints_ref[...].reshape(slots, cells)
    stacked = jnp.concatenate([flat[:, r * width : (r + 1) * width] for r in range(8)], axis=0)
    some = bands // 4
    for turn in range(4):
        at = slice(turn * some, (turn + 1) * some)
        hot = hot_ref[at].reshape(some * 16, slots * 8)
        moved = jnp.dot(hot, stacked, preferred_element_type=jnp.float32).astype(jnp.bfloat16)
        sent_ref[at] = moved.reshape(some, 16, width)
        copies.append(pltpu.make_async_copy(sent_ref.at[at], sent_hbm.at[at], sems.at[2 + turn]))
        copies[-1].start()
    for copy in copies:
        copy.wait()


def edge_kernel(flux_ref, coef_ref, away_ref, beside_ref):
    samples, rows, _ = flux_ref.shape
    core = lax.rem(lax.axis_index("station"), 2)

    def fill(ref, low):
        ref[0:samples] = flux_ref[:, low : low + HALO]
        coef = coef_ref[low : low + HALO]
        head = coef.astype(jnp.bfloat16)
        ref[samples] = head
        ref[samples + 1] = (coef - head.astype(jnp.float32)).astype(jnp.bfloat16)

    @pl.when(core == 0)
    def _():
        fill(away_ref, 0)
        fill(beside_ref, rows - HALO)

    @pl.when(core == 1)
    def _():
        fill(away_ref, rows - HALO)
        fill(beside_ref, 0)


def diffuse_kernel(
    steps_hbm, flux_ref, away_ref, beside_ref, coef_ref,
    out0_hbm, out1_hbm, out2_hbm, out3_hbm, steps_ref, even_ref, odd_ref, coefs_ref, out_ref, sems,
):
    steps_in = pltpu.make_async_copy(steps_hbm, steps_ref, sems.at[PARTS])
    steps_in.start()
    own = lax.axis_index("sample")
    core = lax.rem(lax.axis_index("station"), 2)
    samples, rows, lon = flux_ref.shape
    strips = lon // LANES
    tall = rows + 2 * HALO
    edge = jnp.zeros((HALO, LANES), jnp.float32)
    away = pl.multiple_of(core * (HALO + rows), 8)
    near = pl.multiple_of((1 - core) * (HALO + rows), 8)
    lane = lax.broadcasted_iota(jnp.int32, (8, LANES), 1)
    first_lane = lane == 0
    last_lane = lane == LANES - 1

    for strip in range(strips):
        at = slice(strip * LANES, (strip + 1) * LANES)
        for ref, low in ((away_ref, away), (beside_ref, near)):
            coefs_ref[strip, pl.ds(low, HALO)] = ref[samples, :, at].astype(jnp.float32) + ref[
                samples + 1, :, at
            ].astype(jnp.float32)
        coefs_ref[strip, HALO : HALO + rows] = coef_ref[:, at]
        for low in (0, HALO + tall):
            odd_ref[strip, low : low + HALO] = edge
            for sample in range(samples):
                even_ref[sample, strip, low : low + HALO] = edge

    def update(old_ref, new_ref, tile):
        at = HALO + 8 * tile

        def load(strip):
            return old_ref[strip % strips, at : at + 8]

        before = pltpu.roll(load(strips - 1), 1, 1)
        center = load(0)
        ahead = pltpu.roll(center, LANES - 1, 1)
        for strip in range(strips):
            behind = pltpu.roll(center, 1, 1)
            following = load(strip + 1)
            after = pltpu.roll(following, LANES - 1, 1)
            west = jnp.where(first_lane, before, behind)
            east = jnp.where(last_lane, after, ahead)
            north = old_ref[strip, at - 1 : at + 7]
            south = old_ref[strip, at + 1 : at + 9]
            lap = (north + south + east + west) - 4.0 * center
            new_ref[strip, at : at + 8] = center + coefs_ref[strip, 8 * tile : 8 * tile + 8] * lap
            before, center, ahead = behind, following, after

    def step(old_ref, new_ref, last):
        @pl.when(jnp.logical_not(last))
        def _():
            update(old_ref, new_ref, 0)
            update(old_ref, new_ref, tall // 8 - 1)

        for tile in range(1, tall // 8 - 1):
            update(old_ref, new_ref, tile)

    def begin(sample, ref):
        for strip in range(strips):
            at = slice(strip * LANES, (strip + 1) * LANES)
            ref[strip, pl.ds(HALO + away, HALO)] = away_ref[sample, :, at].astype(jnp.float32)
            ref[strip, 2 * HALO : 2 * HALO + rows] = flux_ref[sample, :, at].astype(jnp.float32)
            ref[strip, pl.ds(HALO + near, HALO)] = beside_ref[sample, :, at].astype(jnp.float32)

    def evolve(sample, carry):
        even = even_ref.at[sample]
        count = jnp.minimum(steps_ref[sample], ITERS)
        half = lax.div(count, 2)

        @pl.when(lax.rem(count, 2) == 1)
        def _():
            begin(sample, odd_ref)
            step(odd_ref, even, half == 0)

        @pl.when(lax.rem(count, 2) == 0)
        def _():
            begin(sample, even)

        def two(k, carry):
            step(even, odd_ref, False)
            step(odd_ref, even, k == half - 1)
            return carry

        lax.fori_loop(0, half, two, 0)
        return carry

    steps_in.wait()
    lax.fori_loop(0, samples, evolve, 0)

    copies = []
    for turn, out_hbm in ((2, out2_hbm), (1, out1_hbm), (3, out3_hbm), (0, out0_hbm)):
        low = pl.multiple_of(2 * HALO + 8 * lax.rem(own + turn, PARTS), 8)
        for pair in range(samples // 2):
            for strip in range(strips):
                both = [even_ref[2 * pair + side, strip, pl.ds(low, 8)] for side in range(2)]
                out_ref[turn, 16 * pair : 16 * pair + 16, strip * LANES : (strip + 1) * LANES] = jnp.concatenate(
                    both, axis=0
                ).astype(jnp.bfloat16)
        copies.append(pltpu.make_async_copy(out_ref.at[turn], out_hbm, sems.at[turn]))
        copies[-1].start()
    for copy in copies:
        copy.wait()


def dots_kernel(loc_hbm, prints_ref, *refs):
    parts = refs[:PARTS]
    out_ref, loc_ref, sums_ref, sems = refs[PARTS:]
    loc_in = pltpu.make_async_copy(loc_hbm, loc_ref, sems.at[0])
    loc_in.start()
    bands, _, width = prints_ref.shape
    slots = bands * CAP
    prints = prints_ref[...].reshape(slots * 8, width)
    for low in range(0, TILES_DEV, 2):
        tiles = range(low, min(low + 2, TILES_DEV))
        cells = jnp.concatenate(
            [part[:, tile * width : (tile + 1) * width] for tile in tiles for part in parts], axis=0
        )
        sums = lax.dot_general(prints, cells, (((1,), (1,)), ((), ())), preferred_element_type=jnp.float32)
        for i, tile in enumerate(tiles):
            sums_ref[tile] = sums[:, i * LANES : (i + 1) * LANES].reshape(slots, 8, LANES)
    same = lax.rem(lax.broadcasted_iota(jnp.int32, (8, LANES), 1), 8) == lax.broadcasted_iota(
        jnp.int32, (8, LANES), 0
    )
    shift = 32 * lax.axis_index("sample")
    loc_in.wait()

    def pick(group, carry):
        at = pl.multiple_of(group * 8, 8)
        rows = [
            jnp.sum(jnp.where(same, sums_ref[loc_ref[at + i], at + i], 0.0), axis=0, keepdims=True) for i in range(8)
        ]
        out_ref[pl.ds(at, 8)] = pltpu.roll(jnp.concatenate(rows, axis=0), shift, 1)
        return carry

    lax.fori_loop(0, slots // 8, pick, 0, unroll=2)


def station_kernel(place_ref, count_ref, back_ref, out_ref, sums_ref):
    stations = sums_ref.shape[0]
    for station in range(stations):
        total = back_ref[pl.ds(place_ref[KT * station], 1)]
        for k in range(1, KT):
            row = back_ref[pl.ds(place_ref[KT * station + k], 1)]
            total = total + jnp.where(k < count_ref[station], row, 0.0)
        sums_ref[station : station + 1] = jnp.where(0 < count_ref[station], total, 0.0)
    lane = lax.broadcasted_iota(jnp.int32, (LANES, 16), 0)
    sample = lax.broadcasted_iota(jnp.int32, (LANES, 16), 1)
    fold = (lax.div(lane, 8) == sample).astype(jnp.float32)
    out_ref[...] = jnp.dot(
        sums_ref[...], fold, precision=lax.Precision.HIGHEST, preferred_element_type=jnp.float32
    )


def body(flux, coeff, diff_steps, footprint, tile_src, tile_local, tile_count):
    samples, rows, lon = flux.shape
    stations = footprint.shape[0]
    slots = stations * KT
    bands = lax.axis_size("station")
    band = lax.axis_index("station")
    cells = rows * TILE_LON // PARTS
    across = [(i, i + 1) for i in range(1, bands - 1, 2)] + [(i, i - 1) for i in range(2, bands, 2)]
    within = [(i, i ^ 1) for i in range(bands)]

    away, beside = pl.pallas_call(
        edge_kernel,
        out_shape=[VMEM((samples + 2, HALO, lon), jnp.bfloat16)] * 2,
        in_specs=[spec(VMEM)] * 2,
        out_specs=[spec(VMEM)] * 2,
        name="edges",
    )(flux, coeff)
    away = lax.ppermute(away, "station", across)
    beside = lax.ppermute(beside, "station", within)

    src_all = tile_src[:, :, 0].T
    sent, place = pl.pallas_call(
        pack_kernel,
        out_shape=(
            HBM((bands, 8 * CAP, TILE_LON), jnp.bfloat16),
            HBM((slots,), jnp.int32),
        ),
        in_specs=[spec(HBM), spec(HBM)],
        out_specs=(spec(HBM), spec(HBM)),
        scratch_shapes=[
            SMEM((slots,), jnp.int32),
            SMEM((KT, 1, LANES), jnp.int32),
            SMEM((bands,), jnp.int32),
            SMEM((CAP * bands,), jnp.int32),
            VMEM((stations, KT, cells), jnp.bfloat16),
            VMEM((bands, 8 * CAP, 8 * slots), jnp.bfloat16),
            VMEM((bands, 8 * CAP, TILE_LON), jnp.bfloat16),
            pltpu.SemaphoreType.DMA((7,)),
        ],
        compiler_params=pltpu.CompilerParams(vmem_limit_bytes=24 * 2**20),
        name="pack",
    )(
        pltpu.with_memory_space_constraint(tile_src.transpose(1, 2, 0), HBM),
        pltpu.with_memory_space_constraint(footprint, HBM),
    )
    sent, _, _ = lax.optimization_barrier((sent, away, beside))
    arrived = lax.all_to_all(sent, "station", split_axis=0, concat_axis=0, tiled=True)

    finals = pl.pallas_call(
        diffuse_kernel,
        out_shape=[jax.ShapeDtypeStruct((samples * 8, lon), jnp.bfloat16)]
        + [HBM((samples * 8, lon), jnp.bfloat16)] * (PARTS - 1),
        in_specs=[spec(HBM)] + [spec(VMEM)] * 4,
        out_specs=[spec(HBM)] * PARTS,
        scratch_shapes=[
            SMEM((samples,), jnp.int32),
            VMEM((samples, lon // LANES, rows + 4 * HALO, LANES), jnp.float32),
            VMEM((lon // LANES, rows + 4 * HALO, LANES), jnp.float32),
            VMEM((lon // LANES, rows + 2 * HALO, LANES), jnp.float32),
            VMEM((PARTS, samples * 8, lon), jnp.bfloat16),
            pltpu.SemaphoreType.DMA((PARTS + 1,)),
        ],
        compiler_params=pltpu.CompilerParams(vmem_limit_bytes=24 * 2**20),
        name="diffuse",
    )(diff_steps, flux, away, beside, coeff)
    parts = [finals[0]] + [
        lax.ppermute(finals[turn], "sample", [(i, (i + turn) % PARTS) for i in range(PARTS)]) for turn in (3, 2, 1)
    ]

    local, _ = lax.optimization_barrier((tile_local, finals[0]))
    order = jnp.arange(stations * bands, dtype=jnp.int32) % stations
    code = (order[None, :] * KT + jnp.arange(KT, dtype=jnp.int32)[:, None]) * 8 + local.T
    named = src_all == band
    first = jnp.min(jnp.min(jnp.where(named, code, slots * 8), axis=0).reshape(bands, stations), axis=1)
    last = jnp.max(jnp.max(jnp.where(named, code, 0), axis=0).reshape(bands, stations), axis=1)
    loc = jnp.stack([first & 7, last & 7], axis=1)

    parts = [pltpu.with_memory_space_constraint(each, VMEM) for each in parts]
    values = pl.pallas_call(
        dots_kernel,
        out_shape=jax.ShapeDtypeStruct((bands * CAP, LANES), jnp.float32),
        in_specs=[spec(HBM)] + [spec(VMEM)] * (1 + PARTS),
        out_specs=spec(VMEM),
        scratch_shapes=[
            SMEM((bands * CAP,), jnp.int32),
            VMEM((TILES_DEV, bands * CAP, 8, LANES), jnp.float32),
            pltpu.SemaphoreType.DMA((1,)),
        ],
        compiler_params=pltpu.CompilerParams(vmem_limit_bytes=24 * 2**20),
        name="dots",
    )(loc.reshape(-1), arrived, *parts)

    back = lax.all_to_all(values.reshape(bands, CAP, LANES), "station", split_axis=0, concat_axis=0, tiled=True)
    back = pltpu.with_memory_space_constraint(back.reshape(bands * CAP, LANES), VMEM)
    share = pl.pallas_call(
        station_kernel,
        out_shape=VMEM((stations, 16), jnp.float32),
        in_specs=[spec(SMEM), spec(SMEM), spec(VMEM)],
        out_specs=spec(VMEM),
        scratch_shapes=[VMEM((stations, LANES), jnp.float32)],
        name="stations",
    )(place, tile_count, back)
    others = [lax.ppermute(share, "sample", [(i, i ^ flip) for i in range(PARTS)]) for flip in (1, 2, 3)]
    return (share + others[0]) + (others[1] + others[2])


def solution(mesh):
    in_specs = (
        P("sample", "station", None),
        P("station", None),
        P("sample"),
        P("station", None, None),
        P(),
        P(),
        P("station"),
    )
    return jax.shard_map(body, mesh=mesh, in_specs=in_specs, out_specs=P("station", None), check_vma=False)
```

```python
import jax
import jax.numpy as jnp
from jax import lax
from jax.experimental import pallas as pl
from jax.experimental.pallas import tpu as pltpu
from jax.sharding import PartitionSpec as P

TILE_LON = 512
TILES_DEV = 7
KT = 4
ITERS = 6
CAP = 2
HALO = 8
PARTS = 4
LANES = 128
VMEM = pltpu.VMEM
SMEM = pltpu.SMEM
HBM = pltpu.HBM


def spec(space):
    return pl.BlockSpec(memory_space=space)


def pack_kernel(
    src_hbm, prints_hbm, sent_hbm, place_hbm,
    place_ref, src_ref, held_ref, slot_ref, prints_ref, hot_ref, sent_ref, sems,
):
    bands, _, width = sent_ref.shape
    stations, _, cells = prints_ref.shape
    slots = stations * KT
    low = pl.multiple_of(lax.axis_index("sample") * cells, cells)
    prints_in = pltpu.make_async_copy(prints_hbm.at[:, :, pl.ds(low, cells)], prints_ref, sems.at[0])
    prints_in.start()
    first = lax.axis_index("station") * stations
    low = pl.multiple_of(lax.div(first, LANES) * LANES, LANES)
    src_in = pltpu.make_async_copy(src_hbm.at[:, :, pl.ds(low, LANES)], src_ref, sems.at[1])
    src_in.start()
    first = lax.rem(first, LANES)

    def clear(i, carry):
        held_ref[i] = 0
        for rank in range(CAP):
            slot_ref[CAP * i + rank] = -(1 << 20)
        return carry

    lax.fori_loop(0, bands, clear, 0, unroll=8)
    src_in.wait()

    def assign(station, carry):
        for k in range(KT):
            band = src_ref[k, 0, first + station]
            rank = jnp.minimum(held_ref[band], CAP - 1)
            held_ref[band] = rank + 1
            place_ref[KT * station + k] = CAP * band + rank
            slot_ref[CAP * band + rank] = KT * station + k
        return carry

    lax.fori_loop(0, stations, assign, 0)
    copies = [pltpu.make_async_copy(place_ref, place_hbm, sems.at[6])]
    copies[0].start()

    row = lax.broadcasted_iota(jnp.int32, (8, width), 0)
    offset = lax.broadcasted_iota(jnp.int32, (8, width), 1) - slots * row

    def heat(i, carry):
        rows = [jnp.where(offset == slot_ref[CAP * i + rank], 1.0, 0.0) for rank in range(CAP)]
        hot_ref[i] = jnp.concatenate(rows, axis=0).astype(jnp.bfloat16)
        return carry

    lax.fori_loop(0, bands, heat, 0, unroll=8)

    prints_in.wait()
    flat = prints_ref[...].reshape(slots, cells)
    stacked = jnp.concatenate([flat[:, r * width : (r + 1) * width] for r in range(8)], axis=0)
    some = bands // 4
    for turn in range(4):
        at = slice(turn * some, (turn + 1) * some)
        hot = hot_ref[at].reshape(some * 16, slots * 8)
        moved = jnp.dot(hot, stacked, preferred_element_type=jnp.float32).astype(jnp.bfloat16)
        sent_ref[at] = moved.reshape(some, 16, width)
        copies.append(pltpu.make_async_copy(sent_ref.at[at], sent_hbm.at[at], sems.at[2 + turn]))
        copies[-1].start()
    for copy in copies:
        copy.wait()


def edge_kernel(flux_ref, coef_ref, away_ref, beside_ref):
    samples, rows, _ = flux_ref.shape
    core = lax.rem(lax.axis_index("station"), 2)

    def fill(ref, low):
        ref[0:samples] = flux_ref[:, low : low + HALO]
        coef = coef_ref[low : low + HALO]
        head = coef.astype(jnp.bfloat16)
        ref[samples] = head
        ref[samples + 1] = (coef - head.astype(jnp.float32)).astype(jnp.bfloat16)

    @pl.when(core == 0)
    def _():
        fill(away_ref, 0)
        fill(beside_ref, rows - HALO)

    @pl.when(core == 1)
    def _():
        fill(away_ref, rows - HALO)
        fill(beside_ref, 0)


def diffuse_kernel(
    steps_hbm, flux_ref, away_ref, beside_ref, coef_ref,
    out0_hbm, out1_hbm, out2_hbm, out3_hbm, steps_ref, even_ref, odd_ref, coefs_ref, out_ref, sems,
):
    steps_in = pltpu.make_async_copy(steps_hbm, steps_ref, sems.at[PARTS])
    steps_in.start()
    own = lax.axis_index("sample")
    core = lax.rem(lax.axis_index("station"), 2)
    samples, rows, lon = flux_ref.shape
    strips = lon // LANES
    tall = rows + 2 * HALO
    edge = jnp.zeros((HALO, LANES), jnp.float32)
    away = pl.multiple_of(core * (HALO + rows), 8)
    near = pl.multiple_of((1 - core) * (HALO + rows), 8)
    lane = lax.broadcasted_iota(jnp.int32, (8, LANES), 1)
    first_lane = lane == 0
    last_lane = lane == LANES - 1

    for strip in range(strips):
        at = slice(strip * LANES, (strip + 1) * LANES)
        for ref, low in ((away_ref, away), (beside_ref, near)):
            coefs_ref[strip, pl.ds(low, HALO)] = ref[samples, :, at].astype(jnp.float32) + ref[
                samples + 1, :, at
            ].astype(jnp.float32)
        coefs_ref[strip, HALO : HALO + rows] = coef_ref[:, at]
        for low in (0, HALO + tall):
            odd_ref[strip, low : low + HALO] = edge
            for sample in range(samples):
                even_ref[sample, strip, low : low + HALO] = edge

    def update(old_ref, new_ref, tile):
        at = HALO + 8 * tile

        def load(strip):
            return old_ref[strip % strips, at : at + 8]

        before = pltpu.roll(load(strips - 1), 1, 1)
        center = load(0)
        ahead = pltpu.roll(center, LANES - 1, 1)
        for strip in range(strips):
            behind = pltpu.roll(center, 1, 1)
            following = load(strip + 1)
            after = pltpu.roll(following, LANES - 1, 1)
            west = jnp.where(first_lane, before, behind)
            east = jnp.where(last_lane, after, ahead)
            north = old_ref[strip, at - 1 : at + 7]
            south = old_ref[strip, at + 1 : at + 9]
            lap = (north + south + east + west) - 4.0 * center
            new_ref[strip, at : at + 8] = center + coefs_ref[strip, 8 * tile : 8 * tile + 8] * lap
            before, center, ahead = behind, following, after

    def step(old_ref, new_ref, last):
        @pl.when(jnp.logical_not(last))
        def _():
            update(old_ref, new_ref, 0)
            update(old_ref, new_ref, tall // 8 - 1)

        for tile in range(1, tall // 8 - 1):
            update(old_ref, new_ref, tile)

    def begin(sample, ref):
        for strip in range(strips):
            at = slice(strip * LANES, (strip + 1) * LANES)
            ref[strip, pl.ds(HALO + away, HALO)] = away_ref[sample, :, at].astype(jnp.float32)
            ref[strip, 2 * HALO : 2 * HALO + rows] = flux_ref[sample, :, at].astype(jnp.float32)
            ref[strip, pl.ds(HALO + near, HALO)] = beside_ref[sample, :, at].astype(jnp.float32)

    def evolve(sample, carry):
        even = even_ref.at[sample]
        count = jnp.minimum(steps_ref[sample], ITERS)
        half = lax.div(count, 2)

        @pl.when(lax.rem(count, 2) == 1)
        def _():
            begin(sample, odd_ref)
            step(odd_ref, even, half == 0)

        @pl.when(lax.rem(count, 2) == 0)
        def _():
            begin(sample, even)

        def two(k, carry):
            step(even, odd_ref, False)
            step(odd_ref, even, k == half - 1)
            return carry

        lax.fori_loop(0, half, two, 0)
        return carry

    steps_in.wait()
    lax.fori_loop(0, samples, evolve, 0)

    copies = []
    for turn, out_hbm in ((2, out2_hbm), (1, out1_hbm), (3, out3_hbm), (0, out0_hbm)):
        low = pl.multiple_of(2 * HALO + 8 * (own ^ turn), 8)
        for pair in range(samples // 2):
            for strip in range(strips):
                both = [even_ref[2 * pair + side, strip, pl.ds(low, 8)] for side in range(2)]
                out_ref[turn, 16 * pair : 16 * pair + 16, strip * LANES : (strip + 1) * LANES] = jnp.concatenate(
                    both, axis=0
                ).astype(jnp.bfloat16)
        copies.append(pltpu.make_async_copy(out_ref.at[turn], out_hbm, sems.at[turn]))
        copies[-1].start()
    for copy in copies:
        copy.wait()


def dots_kernel(loc_hbm, prints_ref, *refs):
    parts = refs[:PARTS]
    out_ref, loc_ref, sums_ref, sems = refs[PARTS:]
    loc_in = pltpu.make_async_copy(loc_hbm, loc_ref, sems.at[0])
    loc_in.start()
    bands, _, width = prints_ref.shape
    slots = bands * CAP
    prints = prints_ref[...].reshape(slots * 8, width)
    for low in range(0, TILES_DEV, 2):
        tiles = range(low, min(low + 2, TILES_DEV))
        cells = jnp.concatenate(
            [part[:, tile * width : (tile + 1) * width] for tile in tiles for part in parts], axis=0
        )
        sums = lax.dot_general(prints, cells, (((1,), (1,)), ((), ())), preferred_element_type=jnp.float32)
        for i, tile in enumerate(tiles):
            sums_ref[tile] = sums[:, i * LANES : (i + 1) * LANES].reshape(slots, 8, LANES)
    same = lax.rem(lax.broadcasted_iota(jnp.int32, (8, LANES), 1), 8) == lax.broadcasted_iota(
        jnp.int32, (8, LANES), 0
    )
    own = lax.axis_index("sample")
    odd_block = lax.rem(lax.div(lax.broadcasted_iota(jnp.int32, (8, LANES), 1), 32), 2) == 1
    loc_in.wait()

    def pick(group, carry):
        at = pl.multiple_of(group * 8, 8)
        rows = [
            jnp.sum(jnp.where(same, sums_ref[loc_ref[at + i], at + i], 0.0), axis=0, keepdims=True) for i in range(8)
        ]
        found = jnp.concatenate(rows, axis=0)
        swapped = jnp.where(odd_block, pltpu.roll(found, 32, 1), pltpu.roll(found, LANES - 32, 1))
        found = jnp.where((own & 1) == 1, swapped, found)
        out_ref[pl.ds(at, 8)] = jnp.where((own & 2) == 2, pltpu.roll(found, 64, 1), found)
        return carry

    lax.fori_loop(0, slots // 8, pick, 0, unroll=2)


def station_kernel(place_ref, count_ref, back_ref, out_ref, sums_ref):
    stations = sums_ref.shape[0]
    for station in range(stations):
        total = back_ref[pl.ds(place_ref[KT * station], 1)]
        for k in range(1, KT):
            row = back_ref[pl.ds(place_ref[KT * station + k], 1)]
            total = total + jnp.where(k < count_ref[station], row, 0.0)
        sums_ref[station : station + 1] = jnp.where(0 < count_ref[station], total, 0.0)
    lane = lax.broadcasted_iota(jnp.int32, (LANES, 16), 0)
    sample = lax.broadcasted_iota(jnp.int32, (LANES, 16), 1)
    fold = (lax.div(lane, 8) == sample).astype(jnp.float32)
    out_ref[...] = jnp.dot(
        sums_ref[...], fold, precision=lax.Precision.HIGHEST, preferred_element_type=jnp.float32
    )


def body(flux, coeff, diff_steps, footprint, tile_src, tile_local, tile_count):
    samples, rows, lon = flux.shape
    stations = footprint.shape[0]
    slots = stations * KT
    bands = lax.axis_size("station")
    band = lax.axis_index("station")
    cells = rows * TILE_LON // PARTS
    across = [(i, i + 1) for i in range(1, bands - 1, 2)] + [(i, i - 1) for i in range(2, bands, 2)]
    within = [(i, i ^ 1) for i in range(bands)]

    away, beside = pl.pallas_call(
        edge_kernel,
        out_shape=[VMEM((samples + 2, HALO, lon), jnp.bfloat16)] * 2,
        in_specs=[spec(VMEM)] * 2,
        out_specs=[spec(VMEM)] * 2,
        name="edges",
    )(flux, coeff)
    away = lax.ppermute(away, "station", across)
    beside = lax.ppermute(beside, "station", within)

    src_all = tile_src[:, :, 0].T
    sent, place = pl.pallas_call(
        pack_kernel,
        out_shape=(
            HBM((bands, 8 * CAP, TILE_LON), jnp.bfloat16),
            HBM((slots,), jnp.int32),
        ),
        in_specs=[spec(HBM), spec(HBM)],
        out_specs=(spec(HBM), spec(HBM)),
        scratch_shapes=[
            SMEM((slots,), jnp.int32),
            SMEM((KT, 1, LANES), jnp.int32),
            SMEM((bands,), jnp.int32),
            SMEM((CAP * bands,), jnp.int32),
            VMEM((stations, KT, cells), jnp.bfloat16),
            VMEM((bands, 8 * CAP, 8 * slots), jnp.bfloat16),
            VMEM((bands, 8 * CAP, TILE_LON), jnp.bfloat16),
            pltpu.SemaphoreType.DMA((7,)),
        ],
        compiler_params=pltpu.CompilerParams(vmem_limit_bytes=24 * 2**20),
        name="pack",
    )(
        pltpu.with_memory_space_constraint(tile_src.transpose(1, 2, 0), HBM),
        pltpu.with_memory_space_constraint(footprint, HBM),
    )
    sent, _, _ = lax.optimization_barrier((sent, away, beside))
    arrived = lax.all_to_all(sent, "station", split_axis=0, concat_axis=0, tiled=True)

    finals = pl.pallas_call(
        diffuse_kernel,
        out_shape=[jax.ShapeDtypeStruct((samples * 8, lon), jnp.bfloat16)]
        + [HBM((samples * 8, lon), jnp.bfloat16)] * (PARTS - 1),
        in_specs=[spec(HBM)] + [spec(VMEM)] * 4,
        out_specs=[spec(HBM)] * PARTS,
        scratch_shapes=[
            SMEM((samples,), jnp.int32),
            VMEM((samples, lon // LANES, rows + 4 * HALO, LANES), jnp.float32),
            VMEM((lon // LANES, rows + 4 * HALO, LANES), jnp.float32),
            VMEM((lon // LANES, rows + 2 * HALO, LANES), jnp.float32),
            VMEM((PARTS, samples * 8, lon), jnp.bfloat16),
            pltpu.SemaphoreType.DMA((PARTS + 1,)),
        ],
        compiler_params=pltpu.CompilerParams(vmem_limit_bytes=24 * 2**20),
        name="diffuse",
    )(diff_steps, flux, away, beside, coeff)
    parts = [finals[0]] + [
        lax.ppermute(finals[turn], "sample", [(i, i ^ turn) for i in range(PARTS)]) for turn in range(1, PARTS)
    ]

    local, _ = lax.optimization_barrier((tile_local, finals[0]))
    order = jnp.arange(stations * bands, dtype=jnp.int32) % stations
    code = (order[None, :] * KT + jnp.arange(KT, dtype=jnp.int32)[:, None]) * 8 + local.T
    named = src_all == band
    first = jnp.min(jnp.min(jnp.where(named, code, slots * 8), axis=0).reshape(bands, stations), axis=1)
    last = jnp.max(jnp.max(jnp.where(named, code, 0), axis=0).reshape(bands, stations), axis=1)
    loc = jnp.stack([first & 7, last & 7], axis=1)

    parts = [pltpu.with_memory_space_constraint(each, VMEM) for each in parts]
    values = pl.pallas_call(
        dots_kernel,
        out_shape=jax.ShapeDtypeStruct((bands * CAP, LANES), jnp.float32),
        in_specs=[spec(HBM)] + [spec(VMEM)] * (1 + PARTS),
        out_specs=spec(VMEM),
        scratch_shapes=[
            SMEM((bands * CAP,), jnp.int32),
            VMEM((TILES_DEV, bands * CAP, 8, LANES), jnp.float32),
            pltpu.SemaphoreType.DMA((1,)),
        ],
        compiler_params=pltpu.CompilerParams(vmem_limit_bytes=24 * 2**20),
        name="dots",
    )(loc.reshape(-1), arrived, *parts)

    back = lax.all_to_all(values.reshape(bands, CAP, LANES), "station", split_axis=0, concat_axis=0, tiled=True)
    back = pltpu.with_memory_space_constraint(back.reshape(bands * CAP, LANES), VMEM)
    share = pl.pallas_call(
        station_kernel,
        out_shape=VMEM((stations, 16), jnp.float32),
        in_specs=[spec(SMEM), spec(SMEM), spec(VMEM)],
        out_specs=spec(VMEM),
        scratch_shapes=[VMEM((stations, LANES), jnp.float32)],
        name="stations",
    )(place, tile_count, back)
    others = [lax.ppermute(share, "sample", [(i, i ^ flip) for i in range(PARTS)]) for flip in (1, 2, 3)]
    return (share + others[0]) + (others[1] + others[2])


def solution(mesh):
    in_specs = (
        P("sample", "station", None),
        P("station", None),
        P("sample"),
        P("station", None, None),
        P(),
        P(),
        P("station"),
    )
    return jax.shard_map(body, mesh=mesh, in_specs=in_specs, out_specs=P("station", None), check_vma=False)
```

```python
import jax
import jax.numpy as jnp
from jax import lax
from jax.experimental import pallas as pl
from jax.experimental.pallas import tpu as pltpu
from jax.sharding import PartitionSpec as P

TILE_LON = 512
TILES_DEV = 7
KT = 4
ITERS = 6
CAP = 2
HALO = 8
PARTS = 4
LANES = 128
VMEM = pltpu.VMEM
SMEM = pltpu.SMEM
HBM = pltpu.HBM


def spec(space):
    return pl.BlockSpec(memory_space=space)


def pack_kernel(
    src_hbm, prints_hbm, sent_hbm, place_hbm,
    place_ref, src_ref, held_ref, slot_ref, prints_ref, hot_ref, sent_ref, sems,
):
    bands, _, width = sent_ref.shape
    stations, _, cells = prints_ref.shape
    slots = stations * KT
    low = pl.multiple_of(lax.axis_index("sample") * cells, cells)
    prints_in = pltpu.make_async_copy(prints_hbm.at[:, :, pl.ds(low, cells)], prints_ref, sems.at[0])
    prints_in.start()
    first = lax.axis_index("station") * stations
    low = pl.multiple_of(lax.div(first, LANES) * LANES, LANES)
    src_in = pltpu.make_async_copy(src_hbm.at[:, :, pl.ds(low, LANES)], src_ref, sems.at[1])
    src_in.start()
    first = lax.rem(first, LANES)

    def clear(i, carry):
        held_ref[i] = 0
        for rank in range(CAP):
            slot_ref[CAP * i + rank] = -(1 << 20)
        return carry

    lax.fori_loop(0, bands, clear, 0, unroll=8)
    src_in.wait()

    def assign(station, carry):
        for k in range(KT):
            band = src_ref[k, 0, first + station]
            rank = jnp.minimum(held_ref[band], CAP - 1)
            held_ref[band] = rank + 1
            place_ref[KT * station + k] = CAP * band + rank
            slot_ref[CAP * band + rank] = KT * station + k
        return carry

    lax.fori_loop(0, stations, assign, 0)
    copies = [pltpu.make_async_copy(place_ref, place_hbm, sems.at[6])]
    copies[0].start()

    row = lax.broadcasted_iota(jnp.int32, (8, width), 0)
    offset = lax.broadcasted_iota(jnp.int32, (8, width), 1) - slots * row

    def heat(i, carry):
        rows = [jnp.where(offset == slot_ref[CAP * i + rank], 1.0, 0.0) for rank in range(CAP)]
        hot_ref[i] = jnp.concatenate(rows, axis=0).astype(jnp.bfloat16)
        return carry

    lax.fori_loop(0, bands, heat, 0, unroll=8)

    prints_in.wait()
    flat = prints_ref[...].reshape(slots, cells)
    stacked = jnp.concatenate([flat[:, r * width : (r + 1) * width] for r in range(8)], axis=0)
    some = bands // 4
    for turn in range(4):
        at = slice(turn * some, (turn + 1) * some)
        hot = hot_ref[at].reshape(some * 16, slots * 8)
        moved = jnp.dot(hot, stacked, preferred_element_type=jnp.float32).astype(jnp.bfloat16)
        sent_ref[at] = moved.reshape(some, 16, width)
        copies.append(pltpu.make_async_copy(sent_ref.at[at], sent_hbm.at[at], sems.at[2 + turn]))
        copies[-1].start()
    for copy in copies:
        copy.wait()


def edge_kernel(flux_ref, coef_ref, away_ref, beside_ref):
    samples, rows, _ = flux_ref.shape
    core = lax.rem(lax.axis_index("station"), 2)

    def fill(ref, low):
        ref[0:samples] = flux_ref[:, low : low + HALO]
        coef = coef_ref[low : low + HALO]
        head = coef.astype(jnp.bfloat16)
        ref[samples] = head
        ref[samples + 1] = (coef - head.astype(jnp.float32)).astype(jnp.bfloat16)

    @pl.when(core == 0)
    def _():
        fill(away_ref, 0)
        fill(beside_ref, rows - HALO)

    @pl.when(core == 1)
    def _():
        fill(away_ref, rows - HALO)
        fill(beside_ref, 0)


def diffuse_kernel(
    steps_hbm, flux_ref, away_ref, beside_ref, coef_ref,
    out0_hbm, out1_hbm, out2_hbm, out3_hbm, steps_ref, even_ref, odd_ref, coefs_ref, out_ref, sems,
):
    steps_in = pltpu.make_async_copy(steps_hbm, steps_ref, sems.at[PARTS])
    steps_in.start()
    own = lax.axis_index("sample")
    core = lax.rem(lax.axis_index("station"), 2)
    samples, rows, lon = flux_ref.shape
    strips = lon // LANES
    tall = rows + 2 * HALO
    edge = jnp.zeros((HALO, LANES), jnp.float32)
    away = pl.multiple_of(core * (HALO + rows), 8)
    near = pl.multiple_of((1 - core) * (HALO + rows), 8)
    lane = lax.broadcasted_iota(jnp.int32, (8, LANES), 1)
    first_lane = lane == 0
    last_lane = lane == LANES - 1

    for strip in range(strips):
        at = slice(strip * LANES, (strip + 1) * LANES)
        for ref, low in ((away_ref, away), (beside_ref, near)):
            coefs_ref[strip, pl.ds(low, HALO)] = ref[samples, :, at].astype(jnp.float32) + ref[
                samples + 1, :, at
            ].astype(jnp.float32)
        coefs_ref[strip, HALO : HALO + rows] = coef_ref[:, at]
        for low in (0, HALO + tall):
            odd_ref[strip, low : low + HALO] = edge
            for sample in range(samples):
                even_ref[sample, strip, low : low + HALO] = edge

    def update(old_ref, new_ref, tile):
        at = HALO + 8 * tile

        def load(strip):
            return old_ref[strip % strips, at : at + 8]

        before = pltpu.roll(load(strips - 1), 1, 1)
        center = load(0)
        ahead = pltpu.roll(center, LANES - 1, 1)
        for strip in range(strips):
            behind = pltpu.roll(center, 1, 1)
            following = load(strip + 1)
            after = pltpu.roll(following, LANES - 1, 1)
            west = jnp.where(first_lane, before, behind)
            east = jnp.where(last_lane, after, ahead)
            north = old_ref[strip, at - 1 : at + 7]
            south = old_ref[strip, at + 1 : at + 9]
            lap = (north + south + east + west) - 4.0 * center
            new_ref[strip, at : at + 8] = center + coefs_ref[strip, 8 * tile : 8 * tile + 8] * lap
            before, center, ahead = behind, following, after

    def step(old_ref, new_ref, last):
        @pl.when(jnp.logical_not(last))
        def _():
            update(old_ref, new_ref, 0)
            update(old_ref, new_ref, tall // 8 - 1)

        for tile in range(1, tall // 8 - 1):
            update(old_ref, new_ref, tile)

    def begin(sample, ref):
        for strip in range(strips):
            at = slice(strip * LANES, (strip + 1) * LANES)
            ref[strip, pl.ds(HALO + away, HALO)] = away_ref[sample, :, at].astype(jnp.float32)
            ref[strip, 2 * HALO : 2 * HALO + rows] = flux_ref[sample, :, at].astype(jnp.float32)
            ref[strip, pl.ds(HALO + near, HALO)] = beside_ref[sample, :, at].astype(jnp.float32)

    def evolve(sample, carry):
        even = even_ref.at[sample]
        count = jnp.minimum(steps_ref[sample], ITERS)
        half = lax.div(count, 2)

        @pl.when(lax.rem(count, 2) == 1)
        def _():
            begin(sample, odd_ref)
            step(odd_ref, even, half == 0)

        @pl.when(lax.rem(count, 2) == 0)
        def _():
            begin(sample, even)

        def two(k, carry):
            step(even, odd_ref, False)
            step(odd_ref, even, k == half - 1)
            return carry

        lax.fori_loop(0, half, two, 0)
        return carry

    steps_in.wait()
    lax.fori_loop(0, samples, evolve, 0)

    copies = []
    for turn, out_hbm in ((2, out2_hbm), (1, out1_hbm), (3, out3_hbm), (0, out0_hbm)):
        low = pl.multiple_of(2 * HALO + 8 * (own ^ turn), 8)
        for pair in range(samples // 2):
            for strip in range(strips):
                both = [even_ref[2 * pair + side, strip, pl.ds(low, 8)] for side in range(2)]
                out_ref[turn, 16 * pair : 16 * pair + 16, strip * LANES : (strip + 1) * LANES] = jnp.concatenate(
                    both, axis=0
                ).astype(jnp.bfloat16)
        copies.append(pltpu.make_async_copy(out_ref.at[turn], out_hbm, sems.at[turn]))
        copies[-1].start()
    for copy in copies:
        copy.wait()


def dots_kernel(loc_hbm, prints_ref, *refs):
    parts = refs[:PARTS]
    out_ref, loc_ref, sums_ref, sems = refs[PARTS:]
    loc_in = pltpu.make_async_copy(loc_hbm, loc_ref, sems.at[0])
    loc_in.start()
    bands, _, width = prints_ref.shape
    slots = bands * CAP
    prints = prints_ref[...].reshape(slots * 8, width)
    for low in range(0, TILES_DEV, 2):
        tiles = range(low, min(low + 2, TILES_DEV))
        cells = jnp.concatenate(
            [part[:, tile * width : (tile + 1) * width] for tile in tiles for part in parts], axis=0
        )
        sums = lax.dot_general(prints, cells, (((1,), (1,)), ((), ())), preferred_element_type=jnp.float32)
        for i, tile in enumerate(tiles):
            sums_ref[tile] = sums[:, i * LANES : (i + 1) * LANES].reshape(slots, 8, LANES)
    same = lax.rem(lax.broadcasted_iota(jnp.int32, (8, LANES), 1), 8) == lax.broadcasted_iota(
        jnp.int32, (8, LANES), 0
    )
    loc_in.wait()

    def pick(group, carry):
        at = pl.multiple_of(group * 8, 8)
        rows = [
            jnp.sum(jnp.where(same, sums_ref[loc_ref[at + i], at + i], 0.0), axis=0, keepdims=True) for i in range(8)
        ]
        out_ref[pl.ds(at, 8)] = jnp.concatenate(rows, axis=0)
        return carry

    lax.fori_loop(0, slots // 8, pick, 0, unroll=2)


def station_kernel(place_ref, count_ref, back_ref, out_ref, sums_ref):
    stations = sums_ref.shape[0]
    for station in range(stations):
        total = back_ref[pl.ds(place_ref[KT * station], 1)]
        for k in range(1, KT):
            row = back_ref[pl.ds(place_ref[KT * station + k], 1)]
            total = total + jnp.where(k < count_ref[station], row, 0.0)
        sums_ref[station : station + 1] = jnp.where(0 < count_ref[station], total, 0.0)
    lane = lax.broadcasted_iota(jnp.int32, (LANES, 16), 0)
    sample = lax.broadcasted_iota(jnp.int32, (LANES, 16), 1)
    own = lax.axis_index("sample")
    fold = ((lax.div(lane, 8) ^ (4 * own)) == sample).astype(jnp.float32)
    out_ref[...] = jnp.dot(
        sums_ref[...], fold, precision=lax.Precision.HIGHEST, preferred_element_type=jnp.float32
    )


def body(flux, coeff, diff_steps, footprint, tile_src, tile_local, tile_count):
    samples, rows, lon = flux.shape
    stations = footprint.shape[0]
    slots = stations * KT
    bands = lax.axis_size("station")
    band = lax.axis_index("station")
    cells = rows * TILE_LON // PARTS
    across = [(i, i + 1) for i in range(1, bands - 1, 2)] + [(i, i - 1) for i in range(2, bands, 2)]
    within = [(i, i ^ 1) for i in range(bands)]

    away, beside = pl.pallas_call(
        edge_kernel,
        out_shape=[VMEM((samples + 2, HALO, lon), jnp.bfloat16)] * 2,
        in_specs=[spec(VMEM)] * 2,
        out_specs=[spec(VMEM)] * 2,
        name="edges",
    )(flux, coeff)
    away = lax.ppermute(away, "station", across)
    beside = lax.ppermute(beside, "station", within)

    src_all = tile_src[:, :, 0].T
    sent, place = pl.pallas_call(
        pack_kernel,
        out_shape=(
            HBM((bands, 8 * CAP, TILE_LON), jnp.bfloat16),
            HBM((slots,), jnp.int32),
        ),
        in_specs=[spec(HBM), spec(HBM)],
        out_specs=(spec(HBM), spec(HBM)),
        scratch_shapes=[
            SMEM((slots,), jnp.int32),
            SMEM((KT, 1, LANES), jnp.int32),
            SMEM((bands,), jnp.int32),
            SMEM((CAP * bands,), jnp.int32),
            VMEM((stations, KT, cells), jnp.bfloat16),
            VMEM((bands, 8 * CAP, 8 * slots), jnp.bfloat16),
            VMEM((bands, 8 * CAP, TILE_LON), jnp.bfloat16),
            pltpu.SemaphoreType.DMA((7,)),
        ],
        compiler_params=pltpu.CompilerParams(vmem_limit_bytes=24 * 2**20),
        name="pack",
    )(
        pltpu.with_memory_space_constraint(tile_src.transpose(1, 2, 0), HBM),
        pltpu.with_memory_space_constraint(footprint, HBM),
    )
    sent, _, _ = lax.optimization_barrier((sent, away, beside))
    arrived = lax.all_to_all(sent, "station", split_axis=0, concat_axis=0, tiled=True)

    finals = pl.pallas_call(
        diffuse_kernel,
        out_shape=[jax.ShapeDtypeStruct((samples * 8, lon), jnp.bfloat16)]
        + [HBM((samples * 8, lon), jnp.bfloat16)] * (PARTS - 1),
        in_specs=[spec(HBM)] + [spec(VMEM)] * 4,
        out_specs=[spec(HBM)] * PARTS,
        scratch_shapes=[
            SMEM((samples,), jnp.int32),
            VMEM((samples, lon // LANES, rows + 4 * HALO, LANES), jnp.float32),
            VMEM((lon // LANES, rows + 4 * HALO, LANES), jnp.float32),
            VMEM((lon // LANES, rows + 2 * HALO, LANES), jnp.float32),
            VMEM((PARTS, samples * 8, lon), jnp.bfloat16),
            pltpu.SemaphoreType.DMA((PARTS + 1,)),
        ],
        compiler_params=pltpu.CompilerParams(vmem_limit_bytes=24 * 2**20),
        name="diffuse",
    )(diff_steps, flux, away, beside, coeff)
    parts = [finals[0]] + [
        lax.ppermute(finals[turn], "sample", [(i, i ^ turn) for i in range(PARTS)]) for turn in range(1, PARTS)
    ]

    local, _ = lax.optimization_barrier((tile_local, finals[0]))
    order = jnp.arange(stations * bands, dtype=jnp.int32) % stations
    code = (order[None, :] * KT + jnp.arange(KT, dtype=jnp.int32)[:, None]) * 8 + local.T
    named = src_all == band
    first = jnp.min(jnp.min(jnp.where(named, code, slots * 8), axis=0).reshape(bands, stations), axis=1)
    last = jnp.max(jnp.max(jnp.where(named, code, 0), axis=0).reshape(bands, stations), axis=1)
    loc = jnp.stack([first & 7, last & 7], axis=1)

    parts = [pltpu.with_memory_space_constraint(each, VMEM) for each in parts]
    values = pl.pallas_call(
        dots_kernel,
        out_shape=jax.ShapeDtypeStruct((bands * CAP, LANES), jnp.float32),
        in_specs=[spec(HBM)] + [spec(VMEM)] * (1 + PARTS),
        out_specs=spec(VMEM),
        scratch_shapes=[
            SMEM((bands * CAP,), jnp.int32),
            VMEM((TILES_DEV, bands * CAP, 8, LANES), jnp.float32),
            pltpu.SemaphoreType.DMA((1,)),
        ],
        compiler_params=pltpu.CompilerParams(vmem_limit_bytes=24 * 2**20),
        name="dots",
    )(loc.reshape(-1), arrived, *parts)

    back = lax.all_to_all(values.reshape(bands, CAP, LANES), "station", split_axis=0, concat_axis=0, tiled=True)
    back = pltpu.with_memory_space_constraint(back.reshape(bands * CAP, LANES), VMEM)
    share = pl.pallas_call(
        station_kernel,
        out_shape=VMEM((stations, 16), jnp.float32),
        in_specs=[spec(SMEM), spec(SMEM), spec(VMEM)],
        out_specs=spec(VMEM),
        scratch_shapes=[VMEM((stations, LANES), jnp.float32)],
        name="stations",
    )(place, tile_count, back)
    others = [lax.ppermute(share, "sample", [(i, i ^ flip) for i in range(PARTS)]) for flip in (1, 2, 3)]
    return (share + others[0]) + (others[1] + others[2])


def solution(mesh):
    in_specs = (
        P("sample", "station", None),
        P("station", None),
        P("sample"),
        P("station", None, None),
        P(),
        P(),
        P("station"),
    )
    return jax.shard_map(body, mesh=mesh, in_specs=in_specs, out_specs=P("station", None), check_vma=False)
```
